512 devices in a mesh: dp: 32 (over z, core), rep: 16 (over y, x).
Axes of the slice: x: 4, y: 4, z: 16, core: 2. Of those that a mesh axis runs over, the one named last changes fastest.
Arguments:
- layer_input: bfloat16 [4, 1024, 4096], P(None, ('rep', 'dp')), parts along dimension 1, may hold values from -6 to 6
- queries: bfloat16 [4, 1024, 4096], P(None, ('rep', 'dp')), parts along dimension 1, may hold values from -160 to 160
- new_keys: bfloat16 [4, 1024, 512], P(None, ('rep', 'dp')), parts along dimension 1, may hold values from -8 to 8
- new_values: bfloat16 [4, 1024, 512], P(None, ('rep', 'dp')), parts along dimension 1, may hold values from -6 to 6
- key_cache: bfloat16 [16384, 32, 512], P(('rep', 'dp')), parts along dimension 0, may hold values from -6 to 6
- value_cache: bfloat16 [16384, 32, 512], P(('rep', 'dp')), parts along dimension 0, may hold values from -6 to 6
- norm_gain: float32 [4096], replicated, may hold values from 0.5 to 1.5
- gate_weight: bfloat16 [4096, 14336], P(None, 'dp'), may hold values from -0.09375 to 0.09375
- up_weight: bfloat16 [4096, 14336], P(None, 'dp'), may hold values from -0.09375 to 0.09375
- down_weight: bfloat16 [14336, 4096], P('dp'), may hold values from -0.046875 to 0.046875
- batch_sizes: int32 [512], P(('rep', 'dp')), parts along dimension 0, may hold values from 1 to 2, as said below
- cache_lengths: int32 [1024], P(('rep', 'dp')), parts along dimension 0, may hold values from 1 to 512, as said below
- page_table: int32 [1024, 16], P(('rep', 'dp')), parts along dimension 0, may hold values from 0 to 31, as said below
Outputs:
- layer_output: bfloat16 [4, 1024, 4096], P(None, ('rep', 'dp')), parts along dimension 1
The draws below stay inside these ranges and needn't reach their ends.
There are 16 independent parts, one for each index of `rep`. The reference program is written for one: setup_inputs(seed, part) draws one part's arguments, and reference() takes and returns one part's arrays. A program takes and returns all parts, laid end to end along the dimension named above; an argument that names none is the same for every part. Nothing has to cross between parts.
Inputs may be any that keep to these rules, and one draw needn't show every extreme that they name: `batch_sizes`: one rank has exactly 2 live sequences. `cache_lengths`: some live slot holds exactly 512 cached tokens. `page_table`: entries index the owning rank's pool; no pool page appears twice within one rank.
All inputs are finite; a program needn't handle non-finite values.
Results may differ from the reference program's by a relative error of at most 0.019.
Values may be sent and summed in bfloat16 or wider, within the bound.
A program may use at most 64 MiB of HBM per device.

```python
import jax
import jax.numpy as jnp
from jax import lax

D = 4096
H = 32
KVH = 4
HD = 128
FF = 14336
STEPS = 4
PAGE = 32
PMAX = 16
BMAX = 2
NPAGE = 32
ROWS = 64
N_DP = 32


def shared_vectors(key):
    noise = jax.random.normal(jax.random.fold_in(key, 102), (STEPS, BMAX * N_DP, KVH * HD), jnp.float32)
    return noise


def draw_new_keys(key, part):
    noise = shared_vectors(key)
    values = noise
    return jnp.clip(values, -8.0, 8.0).astype(jnp.bfloat16)


def draw_queries(key, part):
    key = jax.random.fold_in(key, 4)
    fresh = jax.random.normal(key, (STEPS, BMAX * N_DP, H * HD), jnp.float32)
    values = fresh
    return jnp.clip(values, -160.0, 160.0).astype(jnp.bfloat16)


def draw_batch_sizes(key, part):
    key = jax.random.fold_in(key, 6)
    sizes = jax.random.randint(key, (N_DP,), 1, BMAX + 1, jnp.int32)
    chosen = jax.random.randint(jax.random.fold_in(key, 1), (), 0, N_DP, jnp.int32)
    return jnp.where(jnp.arange(N_DP, dtype=jnp.int32) == chosen, BMAX, sizes).astype(jnp.int32)


def draw_cache_lengths(key, part):
    key = jax.random.fold_in(key, 7)
    longest = PMAX * PAGE
    raw = jax.random.randint(jax.random.fold_in(key, 1), (BMAX * N_DP,), 1, longest + 1, jnp.int32)
    shifts = jax.random.randint(jax.random.fold_in(key, 2), (BMAX * N_DP,), 0, 4, jnp.int32)
    lengths = jnp.maximum(raw // jnp.left_shift(jnp.int32(1), shifts), 1)
    chosen = jax.random.randint(jax.random.fold_in(key, 3), (), 0, N_DP, jnp.int32) * BMAX
    return jnp.where(jnp.arange(BMAX * N_DP, dtype=jnp.int32) == chosen, longest, lengths).astype(jnp.int32)


def draw_page_table(key, part):
    key = jax.random.fold_in(key, 8)
    keys = jax.random.split(key, N_DP)
    orders = jax.vmap(lambda single: jax.random.permutation(single, BMAX * PMAX))(keys)
    return orders.reshape(N_DP * BMAX, PMAX).astype(jnp.int32)


def block_scale(own_key, shape, pieces, low, high):
    factor_of = 1.0
    for position, parts in pieces:
        heights = jax.random.uniform(jax.random.fold_in(jax.random.fold_in(own_key, 6), position), (parts,), jnp.float32, low / len(pieces), high / len(pieces))
        factor_of = factor_of * jnp.repeat(jnp.exp(heights), shape[position] // parts).reshape((-1,) + (1,) * (len(shape) - 1 - position))
    return factor_of


def scatter_about(key, dims, scale, reach, shards=(), held_as=jnp.bfloat16):
    values = scale * jax.random.normal(key, dims, jnp.float32)
    if shards:
        values = values * block_scale(key, dims, shards, -0.22, 0.18)
    return jnp.clip(values, -reach, reach).astype(held_as)


def setup_inputs(seed: int = 0, part: int = 0) -> dict:
    key_of = jax.random.split(jax.random.key(seed), 14)
    own_keys = jax.random.split(jax.random.fold_in(key_of[13], part), 14)
    layer_input = scatter_about(own_keys[0], (STEPS, ROWS, D), 1.0, 6.0, ((1, 32),))
    queries = draw_queries(jax.random.fold_in(jax.random.fold_in(key_of[13], part), 71), part)
    new_keys = draw_new_keys(jax.random.fold_in(jax.random.fold_in(key_of[13], part), 71), part)
    new_values = scatter_about(own_keys[3], (STEPS, ROWS, KVH * HD), 1.0, 6.0, ((1, 32),))
    key_cache = scatter_about(own_keys[4], (N_DP * NPAGE, PAGE, KVH * HD), 1.0, 6.0, ((0, 32),))
    value_cache = scatter_about(own_keys[5], (N_DP * NPAGE, PAGE, KVH * HD), 1.0, 6.0, ((0, 32),))
    norm_gain = jnp.clip(1.0 + 0.1 * jax.random.normal(key_of[6], (D,), jnp.float32), 0.5, 1.5)
    gate_weight = scatter_about(key_of[7], (D, FF), D ** -0.5, 0.09375, ((1, 32),))
    up_weight = scatter_about(key_of[8], (D, FF), D ** -0.5, 0.09375, ((1, 32),))
    down_weight = scatter_about(key_of[9], (FF, D), FF ** -0.5, 0.046875, ((0, 32),))
    batch_sizes = draw_batch_sizes(jax.random.fold_in(jax.random.fold_in(key_of[13], part), 71), part)
    cache_lengths = draw_cache_lengths(jax.random.fold_in(jax.random.fold_in(key_of[13], part), 71), part)
    page_table = draw_page_table(jax.random.fold_in(jax.random.fold_in(key_of[13], part), 71), part)
    return {"layer_input": layer_input, "queries": queries, "new_keys": new_keys, "new_values": new_values, "key_cache": key_cache, "value_cache": value_cache, "norm_gain": norm_gain, "gate_weight": gate_weight, "up_weight": up_weight, "down_weight": down_weight, "batch_sizes": batch_sizes, "cache_lengths": cache_lengths, "page_table": page_table}


neg_large = -1e+30
eps = 1e-05

def reference(layer_input, queries, new_keys, new_values, key_cache, value_cache, norm_gain, gate_weight, up_weight, down_weight, batch_sizes, cache_lengths, page_table):
    groups = H // KVH
    extent = PMAX * PAGE
    rows = BMAX * N_DP
    row_ids = jnp.arange(rows, dtype=jnp.int32)
    owner = (row_ids // BMAX).astype(jnp.int32)
    live = row_ids % BMAX < batch_sizes[owner]
    global_pages = (owner[:, None] * NPAGE + page_table).astype(jnp.int32)
    cached_keys = key_cache[global_pages].astype(jnp.float32).reshape(rows, extent, KVH, HD)
    cached_values = value_cache[global_pages].astype(jnp.float32).reshape(rows, extent, KVH, HD)
    query_heads = queries.astype(jnp.float32).reshape(STEPS, rows, KVH, groups, HD)
    fresh_keys = new_keys.astype(jnp.float32).reshape(STEPS, rows, KVH, HD)
    fresh_values = new_values.astype(jnp.float32).reshape(STEPS, rows, KVH, HD)
    scale = 1.0 / jnp.sqrt(jnp.float32(HD))
    cache_scores = jnp.einsum('sbkgd,blkd->sbkgl', query_heads, cached_keys) * scale
    fresh_scores = jnp.einsum('sbkgd,tbkd->sbkgt', query_heads, fresh_keys) * scale
    cache_mask = jnp.arange(extent, dtype=jnp.int32)[None, :] < cache_lengths[:, None]
    step_ids = jnp.arange(STEPS, dtype=jnp.int32)
    fresh_mask = step_ids[None, :] <= step_ids[:, None]
    cache_scores = jnp.where(cache_mask[None, :, None, None, :], cache_scores, neg_large)
    fresh_scores = jnp.where(fresh_mask[:, None, None, None, :], fresh_scores, neg_large)
    scores = jnp.concatenate([cache_scores, fresh_scores], axis=-1)
    highest = lax.optimization_barrier(jnp.max(scores, axis=-1, keepdims=True))
    expo = jnp.exp(scores - highest)
    weights = (expo / lax.optimization_barrier(jnp.sum(expo, axis=-1, keepdims=True))).astype(jnp.bfloat16).astype(jnp.float32)
    mixed = jnp.einsum('sbkgl,blkd->sbkgd', weights[..., :extent], cached_values)
    mixed = mixed + jnp.einsum('sbkgt,tbkd->sbkgd', weights[..., extent:], fresh_values)
    attention = mixed.reshape(STEPS, rows, D).astype(jnp.bfloat16)
    residual = layer_input.astype(jnp.float32) + attention.astype(jnp.float32)
    inverse = lax.rsqrt(lax.optimization_barrier(jnp.mean(residual * residual, axis=-1, keepdims=True)) + eps)
    normed = residual * inverse * norm_gain.astype(jnp.float32)
    normed = jnp.where(live[None, :, None], normed, 0.0).astype(jnp.bfloat16)
    flat = normed.reshape(STEPS * rows, D)
    gate = jnp.dot(flat, gate_weight, preferred_element_type=jnp.float32)
    upward = jnp.dot(flat, up_weight, preferred_element_type=jnp.float32)
    hidden = (jax.nn.silu(gate) * upward).astype(jnp.bfloat16)
    width = FF // N_DP

    def add_group(total, index):
        start = (index * width).astype(jnp.int32)
        columns = lax.dynamic_slice_in_dim(hidden, start, width, 1)
        weights_rows = lax.dynamic_slice_in_dim(down_weight, start, width, 0)
        term = jnp.dot(columns, weights_rows, preferred_element_type=jnp.float32)
        return (total + term.astype(jnp.bfloat16).astype(jnp.float32), None)
    total, unused = lax.scan(add_group, jnp.zeros((STEPS * rows, D), jnp.float32), jnp.arange(N_DP, dtype=jnp.int32))
    ffn = total.reshape(STEPS, rows, D)
    return jnp.where(live[None, :, None], residual + ffn, 0.0).astype(jnp.bfloat16)
```

```python
import jax
import jax.numpy as jnp
from jax import lax
from jax.experimental import pallas as pl
from jax.experimental.pallas import tpu as pltpu
from jax.sharding import PartitionSpec as P

D = 4096
H = 32
KVH = 4
HD = 128
HALF = D // 2
NJ = 2
W = HALF // NJ
NC = 4
CW = HALF // NC
CHIPS = 16
POOL = 1024
KEYS = POOL + 128

masked = -1e30
eps = 1e-05
MESH = pl.DeviceIdType.MESH


def slot_of(offset):
    if offset == 8 or offset == -8:
        return 15
    return 2 * offset if offset >= 0 else -2 * offset - 1


def kernel(
    bs_ref, cl_ref, pt_ref, li_ref, q_ref, nk_ref, nv_ref, gain_ref,
    kc_ref, vc_ref, wg_ref, wu_ref, wd_ref,
    out_ref,
    li, q, nk, nv, gain, kb, vb, wgu, wd, rows, res, gath, acc, hid, own, sibs, sibr,
    sp, sm, rp, rm,
    lsem, ag_send, ag_recv, as_send, as_recv,
    ps_send, ps_recv, ms_send, ms_recv, ss_send, ss_recv,
):
    me = lax.axis_index("dp")
    core = lax.rem(me, 2)
    right = lax.rem(me + 2, 32)
    left = lax.rem(me + 30, 32)
    right2 = lax.rem(me + 4, 32)
    left2 = lax.rem(me + 28, 32)
    sib = me + 1 - 2 * core

    def remote(src, dst, send, recv, dev):
        return pltpu.make_async_remote_copy(
            src_ref=src, dst_ref=dst, send_sem=send, recv_sem=recv,
            device_id={"dp": dev}, device_id_type=MESH,
        )

    barrier = pltpu.get_barrier_semaphore()
    for dev in (left, right, left2, right2, sib):
        pl.semaphore_signal(barrier, inc=1, device_id={"dp": dev}, device_id_type=MESH)

    width = wd.shape[0]
    moves = (
        (nk_ref, nk), (nv_ref, nv), (q_ref, q),
        (kc_ref, kb.at[pl.ds(0, POOL)]), (vc_ref, vb.at[pl.ds(0, POOL)]),
        (li_ref, li), (gain_ref, gain),
        (wg_ref, wgu.at[pl.ds(0, width)]), (wu_ref, wgu.at[pl.ds(width, width)]), (wd_ref, wd),
    )
    loads = [pltpu.make_async_copy(src, dst, lsem.at[i]) for i, (src, dst) in enumerate(moves)]
    for load in loads:
        load.start()

    def stacked(ref, width):
        for s in range(4):
            rows[2 * s : 2 * s + 2, :width] = ref[s].astype(jnp.float32)
        return rows[:, :width]

    col1 = lax.broadcasted_iota(jnp.int32, (1, KEYS), 1)
    page = lax.shift_right_logical(col1, 5)
    off = jnp.bitwise_and(col1, 31)
    slot_bias = []
    for b in range(2):
        count = jnp.zeros((1, KEYS), jnp.int32)
        for i in range(16):
            count = jnp.where(page == pt_ref[b, i], cl_ref[b] - 32 * i, count)
        slot_bias.append(jnp.where(off < count, 0.0, masked))
    row8 = lax.broadcasted_iota(jnp.int32, (8, KEYS), 0)
    col8 = lax.broadcasted_iota(jnp.int32, (8, KEYS), 1) - POOL
    rowb = jnp.bitwise_and(row8, 1)
    bias = jnp.where(
        rowb == 0,
        jnp.broadcast_to(slot_bias[0], (8, KEYS)),
        jnp.broadcast_to(slot_bias[1], (8, KEYS)),
    )
    fresh = (
        (col8 >= 0)
        & (col8 < 8)
        & (jnp.bitwise_and(col8, 1) == rowb)
        & (lax.shift_right_arithmetic(col8, 1) <= lax.shift_right_logical(row8, 1))
    )
    bias = jnp.where(fresh, 0.0, bias)

    for load in loads[:2]:
        load.wait()
    zeros8 = jnp.zeros((8, KVH * HD), jnp.float32)
    kb[pl.ds(POOL, 16)] = jnp.concatenate([stacked(nk, KVH * HD), zeros8], 0).astype(jnp.bfloat16)
    vb[pl.ds(POOL, 16)] = jnp.concatenate([stacked(nv, KVH * HD), zeros8], 0).astype(jnp.bfloat16)
    kb[pl.ds(POOL + 16, 112)] = jnp.zeros((112, KVH * HD), jnp.bfloat16)
    vb[pl.ds(POOL + 16, 112)] = jnp.zeros((112, KVH * HD), jnp.bfloat16)
    loads[2].wait()
    qf = stacked(q, D)
    scale = 1.0 / jnp.sqrt(jnp.float32(HD))
    loads[3].wait()
    heads = []
    for k in range(KVH):
        qk = jnp.concatenate(
            [qf[:, (8 * k + g) * HD : (8 * k + g + 1) * HD] for g in range(8)], 0
        ).astype(jnp.bfloat16)
        scores = lax.dot_general(
            qk, kb[:, k * HD : (k + 1) * HD], (((1,), (1,)), ((), ())),
            preferred_element_type=jnp.float32,
        )
        scores = (scores.reshape(8, 8, KEYS) * scale + bias[None]).reshape(64, KEYS)
        highest = jnp.max(scores, axis=-1, keepdims=True)
        expo = jnp.exp(scores - highest)
        total = jnp.sum(expo, axis=-1, keepdims=True)
        if k == 0:
            loads[4].wait()
        mixed = jnp.dot(
            expo.astype(jnp.bfloat16), vb[:, k * HD : (k + 1) * HD],
            preferred_element_type=jnp.float32,
        ) / total
        heads += [mixed[8 * g : 8 * g + 8] for g in range(8)]
    attention = jnp.concatenate(heads, 1).astype(jnp.bfloat16).astype(jnp.float32)
    loads[5].wait()
    residual = stacked(li, D) + attention
    res[...] = residual
    inverse = lax.rsqrt(jnp.mean(residual * residual, axis=-1, keepdims=True) + eps)
    loads[6].wait()
    normed = residual * inverse * gain[...]
    live = jnp.bitwise_and(lax.broadcasted_iota(jnp.int32, (8, D), 0), 1) < bs_ref[0]
    normed = jnp.where(live, normed, 0.0)
    for c in range(NC):
        both = [normed[:, (2 * c + fold) * CW : (2 * c + fold + 1) * CW] for fold in range(2)]
        gath[0, 0, :, c * CW : (c + 1) * CW] = jnp.concatenate(both, 0).astype(jnp.bfloat16)
    acc[...] = jnp.zeros_like(acc)

    pl.semaphore_wait(barrier, 5)

    def lanes(j):
        return pl.ds(j * W, W)

    def ag(src, dst, j, dev):
        return remote(
            gath.at[0, src, :, lanes(j)], gath.at[0, dst, :, lanes(j)],
            ag_send.at[0], ag_recv.at[dst, j], dev,
        )

    groups = ((0, 1), (1, 4), (5, 4), (9, 4), (13, 3))

    def ag_sib(group):
        part = pl.ds(*groups[group])
        return remote(gath.at[0, part], gath.at[1, part], as_send.at[0], as_recv.at[group], sib)

    def spread(distance, j):
        for sign, one, two in ((-1, right, right2), (1, left, left2)):
            source = slot_of(sign * distance)
            if distance < 6 or (j < NJ // 2) == (sign < 0):
                ag(source, slot_of(sign * (distance + 2)), j, two).start()
            ag(source, slot_of(sign * (distance + 1)), j, one).start()

    def arrive(distance, j):
        for sign, dev in ((-1, right), (1, left)):
            if distance < 8 or (j < NJ // 2) == (sign < 0):
                ag(0, slot_of(sign * distance), j, dev).wait_recv()

    for j in range(NJ):
        spread(0, j)
    ag_sib(0).start()

    def piece(c):
        return pl.ds(c * CW, CW)

    def features(c):
        return pl.ds(c * 2 * CW, 2 * CW)

    def gate_up(half, c):
        block = gath[:, pl.ds(half * 8, 8), :, piece(c)].astype(jnp.float32)
        block = block.reshape(16, 2, 8, CW)
        block = jnp.concatenate([block[:, fold].reshape(128, CW) for fold in range(2)], 1)
        acc[half] += lax.dot_general(
            wgu[:, features(c)], block.astype(jnp.bfloat16), (((1,), (1,)), ((), ())),
            preferred_element_type=jnp.float32,
        )

    def activate(half):
        gate = acc[half, :width]
        value = gate / (1.0 + jnp.exp(-gate)) * acc[half, width:]
        hid[half] = value.T.astype(jnp.bfloat16)

    for stage in range(1, 4):
        for j in range(NJ):
            arrive(2 * stage, j)
            spread(2 * stage, j)
        for j in range(NJ):
            arrive(2 * stage - 1, j)
        ag_sib(stage).start()
    for group in range(3):
        ag_sib(group).wait_recv()
    loads[7].wait()
    loads[8].wait()

    def near(c, carry):
        gate_up(0, c)
        return carry

    lax.fori_loop(0, NC, near, 0)
    activate(0)
    for j in range(NJ):
        arrive(7, j)
        arrive(8, j)
    ag_sib(4).start()
    for group in range(3, 5):
        ag_sib(group).wait_recv()

    def far(c, carry):
        gate_up(1, c)
        return carry

    lax.fori_loop(0, NC, far, 0)
    activate(1)

    loads[9].wait()

    def sib_sum(half, c):
        slots = pl.ds(half * 8, 8)
        return remote(
            sibs.at[slots, :, piece(c)], sibr.at[slots, :, piece(c)],
            ss_send.at[0], ss_recv.at[half, c], sib,
        )

    def down(half, c):
        term = jnp.dot(hid[half], wd[:, features(c)], preferred_element_type=jnp.float32)
        both = [term[:, fold * CW : (fold + 1) * CW].reshape(2, 8, 1, 8, CW) for fold in range(2)]
        both = jnp.concatenate(both, 2).reshape(2, 8, 16, CW)
        sibs[pl.ds(half * 8, 8), :, piece(c)] = both[1].astype(jnp.bfloat16)
        sib_sum(half, c).start()
        own[pl.ds(half * 8, 8), :, piece(c)] = both[0]

    def down_far(c, carry):
        down(1, c)
        return carry

    lax.fori_loop(0, NC, down_far, 0)

    def plus(m, j):
        return remote(
            sp.at[m - 1, :, lanes(j)], rp.at[m - 1, :, lanes(j)],
            ps_send.at[m // 8], ps_recv.at[m - 1, j], right if m % 2 else right2,
        )

    def minus(m, j):
        return remote(
            sm.at[m - 1, :, lanes(j)], rm.at[m - 1, :, lanes(j)],
            ms_send.at[m // 8], ms_recv.at[m - 1, j], left if m % 2 else left2,
        )

    sides = ((1, plus, sp, rp), (-1, minus, sm, rm))

    def pass_on(m, j, arrivals):
        for sign, copy, leaving, arrived in sides:
            if m == 8 and (j < NJ // 2) != (sign > 0):
                continue
            slot = slot_of(sign * m)
            value = own[slot, :, lanes(j)] + sibr[slot, :, lanes(j)].astype(jnp.float32)
            for source in arrivals:
                if source == 8 and (j < NJ // 2) != (sign > 0):
                    continue
                copy(source, j).wait_recv()
                value = value + arrived[source - 1, :, lanes(j)].astype(jnp.float32)
            leaving[m - 1, :, lanes(j)] = value.astype(jnp.bfloat16)
            copy(m, j).start()

    for j in range(NJ):
        for c in range(j * NC // NJ, (j + 1) * NC // NJ):
            sib_sum(1, c).wait_recv()
        pass_on(8, j, ())
        pass_on(7, j, ())
    for j in range(NJ):
        pass_on(5, j, ())
    down(0, 0)
    down(0, 1)
    for j in range(NJ):
        pass_on(6, j, (7, 8))
    down(0, 2)
    down(0, 3)
    for c in range(NC):
        sib_sum(0, c).wait_recv()
    for j in range(NJ):
        pass_on(3, j, ())
    for j in range(NJ):
        pass_on(4, j, (5, 6))
    for j in range(NJ):
        pass_on(1, j, ())
    for j in range(NJ):
        pass_on(2, j, (3, 4))

    alive = jnp.bitwise_and(lax.broadcasted_iota(jnp.int32, (8, CW), 0), 1) < bs_ref[0]
    for j in range(NJ):
        for m in (1, 2):
            plus(m, j).wait_recv()
            minus(m, j).wait_recv()
        for c in range(j * NC // NJ, (j + 1) * NC // NJ):
            value = own[0, :, piece(c)] + sibr[0, :, piece(c)].astype(jnp.float32)
            for m in (1, 2):
                for arrived in (rp, rm):
                    value = value + arrived[m - 1, :, piece(c)].astype(jnp.float32)
            for fold in range(2):
                place = pl.ds((2 * c + fold) * CW, CW)
                done = res[:, place] + value[8 * fold : 8 * fold + 8]
                out_ref[:, place] = jnp.where(alive, done, 0.0).astype(jnp.bfloat16)

    def sent(part, sem):
        remote(part, part, sem, sem, sib).wait_send()

    sent(gath.at[0, pl.ds(1, 15)], ag_send.at[0])
    sent(gath.at[0], as_send.at[0])
    sent(sibs, ss_send.at[0])
    sent(sp.at[7, :, pl.ds(0, HALF // 2)], ps_send.at[1])
    sent(sm.at[7, :, pl.ds(0, HALF // 2)], ms_send.at[1])
    sent(sp.at[pl.ds(0, 7)], ps_send.at[0])
    sent(sm.at[pl.ds(0, 7)], ms_send.at[0])


def local(
    layer_input, queries, new_keys, new_values, key_cache, value_cache, norm_gain,
    gate_weight, up_weight, down_weight, batch_sizes, cache_lengths, page_table,
):
    vmem = pl.BlockSpec(memory_space=pltpu.VMEM)
    smem = pl.BlockSpec(memory_space=pltpu.SMEM)
    hbm = pl.BlockSpec(memory_space=pltpu.HBM)
    width = down_weight.shape[0]
    bf16, f32 = jnp.bfloat16, jnp.float32
    dma = pltpu.SemaphoreType.DMA
    out = pl.pallas_call(
        kernel,
        out_shape=jax.ShapeDtypeStruct((8, D), bf16),
        in_specs=[smem] * 3 + [hbm] * 10,
        out_specs=vmem,
        scratch_shapes=[
            pltpu.VMEM((4, 2, D), bf16),
            pltpu.VMEM((4, 2, D), bf16),
            pltpu.VMEM((4, 2, KVH * HD), bf16),
            pltpu.VMEM((4, 2, KVH * HD), bf16),
            pltpu.VMEM((1, D), f32),
            pltpu.VMEM((KEYS, KVH * HD), bf16),
            pltpu.VMEM((KEYS, KVH * HD), bf16),
            pltpu.VMEM((2 * width, D), bf16),
            pltpu.VMEM((width, D), bf16),
            pltpu.VMEM((8, D), f32),
            pltpu.VMEM((8, D), f32),
            pltpu.VMEM((2, 16, 16, HALF), bf16),
            pltpu.VMEM((2, 2 * width, 128), f32),
            pltpu.VMEM((2, 128, width), bf16),
            pltpu.VMEM((16, 16, HALF), f32),
            pltpu.VMEM((16, 16, HALF), bf16),
            pltpu.VMEM((16, 16, HALF), bf16),
            pltpu.VMEM((8, 16, HALF), bf16),
            pltpu.VMEM((8, 16, HALF), bf16),
            pltpu.VMEM((8, 16, HALF), bf16),
            pltpu.VMEM((8, 16, HALF), bf16),
            dma((10,)),
            dma((1,)),
            dma((16, NJ)),
            dma((1,)),
            dma((5,)),
            dma((2,)),
            dma((8, NJ)),
            dma((2,)),
            dma((8, NJ)),
            dma((1,)),
            dma((2, NC)),
        ],
        compiler_params=pltpu.CompilerParams(
            collective_id=0, has_side_effects=True, vmem_limit_bytes=56 * 1024 * 1024
        ),
    )(
        batch_sizes,
        cache_lengths,
        page_table,
        layer_input,
        queries,
        new_keys,
        new_values,
        norm_gain.reshape(1, D),
        key_cache.reshape(POOL, KVH * HD),
        value_cache.reshape(POOL, KVH * HD),
        gate_weight.T,
        up_weight.T,
        down_weight,
    )
    return out.reshape(4, 2, D)


def solution(mesh):
    placed = (
        P(None, ("rep", "dp"), None),
        P(None, ("rep", "dp"), None),
        P(None, ("rep", "dp"), None),
        P(None, ("rep", "dp"), None),
        P(("rep", "dp"), None, None),
        P(("rep", "dp"), None, None),
        P(),
        P(None, "dp"),
        P(None, "dp"),
        P("dp", None),
        P(("rep", "dp")),
        P(("rep", "dp")),
        P(("rep", "dp"), None),
    )
    return jax.shard_map(
        local, mesh=mesh, in_specs=placed, out_specs=P(None, ("rep", "dp"), None), check_vma=False
    )
```

```python
import jax
import jax.numpy as jnp
from jax import lax
from jax.experimental import pallas as pl
from jax.experimental.pallas import tpu as pltpu
from jax.sharding import PartitionSpec as P

D = 4096
H = 32
KVH = 4
HD = 128
HALF = D // 2
NJ = 2
W = HALF // NJ
NC = 4
CW = HALF // NC
CHIPS = 16
POOL = 1024
KEYS = POOL + 128

PARENT = {1: 0, 2: 0, 3: 2, 4: 2, 5: 4, 6: 4, 7: 6, 8: 6}


def children(m):
    return [n for n in sorted(PARENT, reverse=True) if PARENT[n] == m]


masked = -1e30
eps = 1e-05
MESH = pl.DeviceIdType.MESH


def slot_of(offset):
    if offset == 8 or offset == -8:
        return 15
    return 2 * offset if offset >= 0 else -2 * offset - 1


def kernel(
    bs_in, cl_in, pt_in, li_ref, q_ref, nk_ref, nv_ref, gain_ref,
    kc_ref, vc_ref, wg_ref, wu_ref, wd_ref,
    out_ref,
    bs, cl, pt, li, q, nk, nv, gain, kb, vb, wgu, wd, rows, res, gath, acc, hid, own, sibs, sibr,
    sp, sm, rp, rm,
    lsem, ag_send, ag_recv, as_send, as_recv,
    ps_send, ps_recv, ms_send, ms_recv, ss_send, ss_recv,
):
    me = lax.axis_index("dp")
    core = lax.rem(me, 2)
    steps = sorted({n - m for n, m in PARENT.items()})
    right = {step: lax.rem(me + 2 * step, 32) for step in steps}
    left = {step: lax.rem(me + 32 - 2 * step, 32) for step in steps}
    sib = me + 1 - 2 * core

    def remote(src, dst, send, recv, dev):
        return pltpu.make_async_remote_copy(
            src_ref=src, dst_ref=dst, send_sem=send, recv_sem=recv,
            device_id={"dp": dev}, device_id_type=MESH,
        )

    barrier = pltpu.get_barrier_semaphore()
    partners = [*left.values(), *right.values(), sib]
    for dev in partners:
        pl.semaphore_signal(barrier, inc=1, device_id={"dp": dev}, device_id_type=MESH)

    width = wd.shape[0]
    moves = (
        (bs_in, bs), (cl_in, cl), (pt_in, pt),
        (nk_ref, nk), (nv_ref, nv), (q_ref, q),
        (kc_ref, kb.at[pl.ds(0, POOL)]), (vc_ref, vb.at[pl.ds(0, POOL)]),
        (li_ref, li), (gain_ref, gain),
        (wg_ref, wgu.at[pl.ds(0, width)]), (wu_ref, wgu.at[pl.ds(width, width)]), (wd_ref, wd),
    )
    loads = [pltpu.make_async_copy(src, dst, lsem.at[i]) for i, (src, dst) in enumerate(moves)]
    for load in loads[:10]:
        load.start()

    def stacked(ref, width):
        for s in range(4):
            rows[2 * s : 2 * s + 2, :width] = ref[s].astype(jnp.float32)
        return rows[:, :width]

    for load in loads[:3]:
        load.wait()
    col1 = lax.broadcasted_iota(jnp.int32, (1, KEYS), 1)
    page = lax.shift_right_logical(col1, 5)
    off = jnp.bitwise_and(col1, 31)
    slot_bias = []
    for b in range(2):
        count = jnp.zeros((1, KEYS), jnp.int32)
        for i in range(16):
            count = jnp.where(page == pt[b, i], cl[b] - 32 * i, count)
        slot_bias.append(jnp.where(off < count, 0.0, masked))
    row8 = lax.broadcasted_iota(jnp.int32, (8, KEYS), 0)
    col8 = lax.broadcasted_iota(jnp.int32, (8, KEYS), 1) - POOL
    rowb = jnp.bitwise_and(row8, 1)
    bias = jnp.where(
        rowb == 0,
        jnp.broadcast_to(slot_bias[0], (8, KEYS)),
        jnp.broadcast_to(slot_bias[1], (8, KEYS)),
    )
    fresh = (
        (col8 >= 0)
        & (col8 < 8)
        & (jnp.bitwise_and(col8, 1) == rowb)
        & (lax.shift_right_arithmetic(col8, 1) <= lax.shift_right_logical(row8, 1))
    )
    bias = jnp.where(fresh, 0.0, bias)

    for load in loads[3:5]:
        load.wait()
    zeros8 = jnp.zeros((8, KVH * HD), jnp.float32)
    kb[pl.ds(POOL, 16)] = jnp.concatenate([stacked(nk, KVH * HD), zeros8], 0).astype(jnp.bfloat16)
    vb[pl.ds(POOL, 16)] = jnp.concatenate([stacked(nv, KVH * HD), zeros8], 0).astype(jnp.bfloat16)
    kb[pl.ds(POOL + 16, 112)] = jnp.zeros((112, KVH * HD), jnp.bfloat16)
    vb[pl.ds(POOL + 16, 112)] = jnp.zeros((112, KVH * HD), jnp.bfloat16)
    loads[5].wait()
    qf = stacked(q, D)
    scale = 1.0 / jnp.sqrt(jnp.float32(HD))
    loads[6].wait()
    heads = []
    blank = jnp.zeros((64, HD), jnp.float32)
    for pair in range(KVH // 2):
        both = [
            jnp.concatenate(
                [qf[:, (16 * pair + 8 * i + g) * HD : (16 * pair + 8 * i + g + 1) * HD] for g in range(8)], 0
            )
            for i in range(2)
        ]
        both = jnp.concatenate(
            [jnp.concatenate([both[0], blank], 1), jnp.concatenate([blank, both[1]], 1)], 0
        ).astype(jnp.bfloat16)
        place = slice(2 * pair * HD, 2 * (pair + 1) * HD)
        scores = lax.dot_general(
            both, kb[:, place], (((1,), (1,)), ((), ())), preferred_element_type=jnp.float32
        )
        scores = (scores.reshape(16, 8, KEYS) * scale + bias[None]).reshape(128, KEYS)
        highest = jnp.max(scores, axis=-1, keepdims=True)
        expo = jnp.exp(scores - highest)
        total = jnp.sum(expo, axis=-1, keepdims=True)
        if pair == 0:
            loads[7].wait()
            for load in loads[10:]:
                load.start()
        mixed = jnp.dot(
            expo.astype(jnp.bfloat16), vb[:, place], preferred_element_type=jnp.float32
        ) / total
        for i in range(2):
            heads += [
                mixed[64 * i + 8 * g : 64 * i + 8 * g + 8, i * HD : (i + 1) * HD] for g in range(8)
            ]
    attention = jnp.concatenate(heads, 1).astype(jnp.bfloat16).astype(jnp.float32)
    loads[8].wait()
    residual = stacked(li, D) + attention
    res[...] = residual
    inverse = lax.rsqrt(jnp.mean(residual * residual, axis=-1, keepdims=True) + eps)
    loads[9].wait()
    normed = residual * inverse * gain[...]
    live = jnp.bitwise_and(lax.broadcasted_iota(jnp.int32, (8, D), 0), 1) < bs[0]
    normed = jnp.where(live, normed, 0.0)
    for c in range(NC):
        both = [normed[:, (2 * c + fold) * CW : (2 * c + fold + 1) * CW] for fold in range(2)]
        gath[0, 0, :, c * CW : (c + 1) * CW] = jnp.concatenate(both, 0).astype(jnp.bfloat16)
    pl.semaphore_wait(barrier, len(partners))

    def lanes(j):
        return pl.ds(j * W, W)

    def ag(src, dst, j, dev):
        return remote(
            gath.at[0, src, :, lanes(j)], gath.at[0, dst, :, lanes(j)],
            ag_send.at[0], ag_recv.at[dst, j], dev,
        )

    groups = ((0, 1), (1, 4), (5, 4), (9, 4), (13, 3))

    def ag_sib(group, j):
        part = pl.ds(*groups[group])
        return remote(
            gath.at[0, part, :, lanes(j)], gath.at[1, part, :, lanes(j)],
            as_send.at[0], as_recv.at[group, j], sib,
        )

    def goes(m, j, sign):
        return m < 8 or (j < NJ // 2) == (sign > 0)

    def spread(m, j):
        for n in children(m):
            for sign, devices in ((1, right), (-1, left)):
                if goes(n, j, sign):
                    ag(slot_of(-sign * m), slot_of(-sign * n), j, devices[n - m]).start()

    def arrive(m, j):
        for sign in (1, -1):
            if goes(m, j, sign):
                ag(0, slot_of(-sign * m), j, right[1]).wait_recv()

    for j in range(NJ):
        spread(0, j)
    for j in range(NJ):
        ag_sib(0, j).start()

    def piece(c):
        return pl.ds(c * CW, CW)

    def features(c):
        return pl.ds(c * 2 * CW, 2 * CW)

    def gate_up(half, j):
        block = gath[:, pl.ds(half * 8, 8), :, lanes(j)].astype(jnp.float32)
        block = block.reshape(16, 2, 8, W)
        block = jnp.concatenate(
            [
                block[:, fold, :, c * CW : (c + 1) * CW].reshape(128, CW)
                for c in range(NC // NJ)
                for fold in range(2)
            ],
            1,
        )
        term = lax.dot_general(
            wgu[:, pl.ds(j * 2 * W, 2 * W)], block.astype(jnp.bfloat16),
            (((1,), (1,)), ((), ())), preferred_element_type=jnp.float32,
        )
        if j == 0:
            acc[half] = term
        else:
            acc[half] += term

    def activate(half):
        gate = acc[half, :width]
        value = gate / (1.0 + jnp.exp(-gate)) * acc[half, width:]
        hid[half] = value.T.astype(jnp.bfloat16)

    def sib_sum(half, c):
        slots = pl.ds(half * 8, 8)
        return remote(
            sibs.at[slots, :, piece(c)], sibr.at[slots, :, piece(c)],
            ss_send.at[0], ss_recv.at[half, c], sib,
        )

    def down(half):
        def step(c, carry):
            term = jnp.dot(hid[half], wd[:, features(c)], preferred_element_type=jnp.float32)
            both = [
                term[:, fold * CW : (fold + 1) * CW].reshape(2, 8, 1, 8, CW) for fold in range(2)
            ]
            both = jnp.concatenate(both, 2).reshape(2, 8, 16, CW)
            slots = pl.ds(half * 8, 8)
            sibs[slots, :, piece(c)] = both[1].astype(jnp.bfloat16)
            sib_sum(half, c).start()
            own[slots, :, piece(c)] = both[0]
            return carry

        lax.fori_loop(0, NC, step, 0)

    def plus(m, j):
        return remote(
            sp.at[m - 1, :, lanes(j)], rp.at[m - 1, :, lanes(j)],
            ps_send.at[m // 8], ps_recv.at[m - 1, j], right[m - PARENT[m]],
        )

    def minus(m, j):
        return remote(
            sm.at[m - 1, :, lanes(j)], rm.at[m - 1, :, lanes(j)],
            ms_send.at[m // 8], ms_recv.at[m - 1, j], left[m - PARENT[m]],
        )

    sides = ((1, plus, sp, rp), (-1, minus, sm, rm))

    def pass_on(m, j):
        for sign, copy, leaving, arrived in sides:
            if not goes(m, j, sign):
                continue
            slot = slot_of(sign * m)
            value = own[slot, :, lanes(j)] + sibr[slot, :, lanes(j)].astype(jnp.float32)
            for source in children(m):
                if goes(source, j, sign):
                    copy(source, j).wait_recv()
                    value = value + arrived[source - 1, :, lanes(j)].astype(jnp.float32)
            leaving[m - 1, :, lanes(j)] = value.astype(jnp.bfloat16)
            copy(m, j).start()

    def gathered(group):
        for j in range(NJ):
            ag_sib(group, j).wait_recv()

    for stage in range(1, 4):
        for j in range(NJ):
            arrive(2 * stage, j)
            spread(2 * stage, j)
        for j in range(NJ):
            arrive(2 * stage - 1, j)
            ag_sib(stage, j).start()

    for group in range(3):
        gathered(group)
    loads[10].wait()
    loads[11].wait()
    for j in range(NJ):
        gate_up(0, j)
    activate(0)
    loads[12].wait()
    down(0)

    for j in range(NJ):
        arrive(7, j)
        arrive(8, j)
        ag_sib(4, j).start()
    for c in range(NC):
        sib_sum(0, c).wait_recv()
    for j in range(NJ):
        pass_on(3, j)

    for j in range(NJ):
        for group in (3, 4):
            ag_sib(group, j).wait_recv()
        gate_up(1, j)
    activate(1)
    down(1)
    for j in range(NJ):
        pass_on(1, j)
    for j in range(NJ):
        for c in range(j * NC // NJ, (j + 1) * NC // NJ):
            sib_sum(1, c).wait_recv()
        for m in (8, 7):
            pass_on(m, j)
    for m in (5, 6, 4, 2):
        for j in range(NJ):
            pass_on(m, j)

    alive = jnp.bitwise_and(lax.broadcasted_iota(jnp.int32, (8, CW), 0), 1) < bs[0]
    for j in range(NJ):
        for m in children(0):
            plus(m, j).wait_recv()
            minus(m, j).wait_recv()
        for c in range(j * NC // NJ, (j + 1) * NC // NJ):
            value = own[0, :, piece(c)] + sibr[0, :, piece(c)].astype(jnp.float32)
            for m in children(0):
                for arrived in (rp, rm):
                    value = value + arrived[m - 1, :, piece(c)].astype(jnp.float32)
            for fold in range(2):
                place = pl.ds((2 * c + fold) * CW, CW)
                done = res[:, place] + value[8 * fold : 8 * fold + 8]
                out_ref[:, place] = jnp.where(alive, done, 0.0).astype(jnp.bfloat16)

    def sent(part, sem):
        remote(part, part, sem, sem, sib).wait_send()

    sent(gath.at[0, pl.ds(1, 15)], ag_send.at[0])
    sent(gath.at[0], as_send.at[0])
    sent(sibs, ss_send.at[0])
    sent(sp.at[7, :, pl.ds(0, HALF // 2)], ps_send.at[1])
    sent(sm.at[7, :, pl.ds(0, HALF // 2)], ms_send.at[1])
    sent(sp.at[pl.ds(0, 7)], ps_send.at[0])
    sent(sm.at[pl.ds(0, 7)], ms_send.at[0])


def local(
    layer_input, queries, new_keys, new_values, key_cache, value_cache, norm_gain,
    gate_weight, up_weight, down_weight, batch_sizes, cache_lengths, page_table,
):
    vmem = pl.BlockSpec(memory_space=pltpu.VMEM)
    hbm = pl.BlockSpec(memory_space=pltpu.HBM)
    width = down_weight.shape[0]
    bf16, f32 = jnp.bfloat16, jnp.float32
    dma = pltpu.SemaphoreType.DMA
    out = pl.pallas_call(
        kernel,
        out_shape=pltpu.VMEM((8, D), bf16),
        in_specs=[hbm] * 13,
        out_specs=vmem,
        scratch_shapes=[
            pltpu.SMEM((1,), jnp.int32),
            pltpu.SMEM((2,), jnp.int32),
            pltpu.SMEM((2, 16), jnp.int32),
            pltpu.VMEM((4, 2, D), bf16),
            pltpu.VMEM((4, 2, D), bf16),
            pltpu.VMEM((4, 2, KVH * HD), bf16),
            pltpu.VMEM((4, 2, KVH * HD), bf16),
            pltpu.VMEM((1, D), f32),
            pltpu.VMEM((KEYS, KVH * HD), bf16),
            pltpu.VMEM((KEYS, KVH * HD), bf16),
            pltpu.VMEM((2 * width, D), bf16),
            pltpu.VMEM((width, D), bf16),
            pltpu.VMEM((8, D), f32),
            pltpu.VMEM((8, D), f32),
            pltpu.VMEM((2, 16, 16, HALF), bf16),
            pltpu.VMEM((2, 2 * width, 128), f32),
            pltpu.VMEM((2, 128, width), bf16),
            pltpu.VMEM((16, 16, HALF), f32),
            pltpu.VMEM((16, 16, HALF), bf16),
            pltpu.VMEM((16, 16, HALF), bf16),
            pltpu.VMEM((8, 16, HALF), bf16),
            pltpu.VMEM((8, 16, HALF), bf16),
            pltpu.VMEM((8, 16, HALF), bf16),
            pltpu.VMEM((8, 16, HALF), bf16),
            dma((13,)),
            dma((1,)),
            dma((16, NJ)),
            dma((1,)),
            dma((5, NJ)),
            dma((2,)),
            dma((8, NJ)),
            dma((2,)),
            dma((8, NJ)),
            dma((1,)),
            dma((2, NC)),
        ],
        compiler_params=pltpu.CompilerParams(
            collective_id=0, has_side_effects=True, vmem_limit_bytes=56 * 1024 * 1024
        ),
    )(
        batch_sizes,
        cache_lengths,
        page_table,
        layer_input,
        queries,
        new_keys,
        new_values,
        norm_gain.reshape(1, D),
        key_cache.reshape(POOL, KVH * HD),
        value_cache.reshape(POOL, KVH * HD),
        gate_weight.T,
        up_weight.T,
        down_weight,
    )
    return out.reshape(4, 2, D)


def solution(mesh):
    placed = (
        P(None, ("rep", "dp"), None),
        P(None, ("rep", "dp"), None),
        P(None, ("rep", "dp"), None),
        P(None, ("rep", "dp"), None),
        P(("rep", "dp"), None, None),
        P(("rep", "dp"), None, None),
        P(),
        P(None, "dp"),
        P(None, "dp"),
        P("dp", None),
        P(("rep", "dp")),
        P(("rep", "dp")),
        P(("rep", "dp"), None),
    )
    return jax.shard_map(
        local, mesh=mesh, in_specs=placed, out_specs=P(None, ("rep", "dp"), None), check_vma=False
    )
```

```python
import jax
import jax.numpy as jnp
from jax import lax
from jax.experimental import pallas as pl
from jax.experimental.pallas import tpu as pltpu
from jax.sharding import PartitionSpec as P

D = 4096
H = 32
KVH = 4
HD = 128
HALF = D // 2
NJ = 2
W = HALF // NJ
SCALE = 128
NC = 4
CW = HALF // NC
CHIPS = 16
POOL = 1024
KEYS = POOL + 128

PARENT = {1: 0, 2: 0, 3: 2, 4: 2, 5: 4, 6: 4, 7: 6, 8: 6}


def children(m):
    return [n for n in sorted(PARENT, reverse=True) if PARENT[n] == m]


masked = -1e30
eps = 1e-05
MESH = pl.DeviceIdType.MESH


def slot_of(offset):
    if offset == 8 or offset == -8:
        return 15
    return 2 * offset if offset >= 0 else -2 * offset - 1


def kernel(
    bs_in, cl_in, pt_in, li_ref, q_ref, nk_ref, nv_ref, gain_ref,
    kc_ref, vc_ref, wg_ref, wu_ref, wd_ref,
    out_ref,
    bs, cl, pt, li, q, nk, nv, gain, kb, vb, wgu, wd, rows, res, gath, acc, hid, own, sibs, sibr,
    sp, sm, rp, rm,
    lsem, ag_send, ag_recv, as_send, as_recv,
    ps_send, ps_recv, ms_send, ms_recv, ss_send, ss_recv,
):
    me = lax.axis_index("dp")
    core = lax.rem(me, 2)
    steps = sorted({n - m for n, m in PARENT.items()})
    right = {step: lax.rem(me + 2 * step, 32) for step in steps}
    left = {step: lax.rem(me + 32 - 2 * step, 32) for step in steps}
    sib = me + 1 - 2 * core

    def remote(src, dst, send, recv, dev):
        return pltpu.make_async_remote_copy(
            src_ref=src, dst_ref=dst, send_sem=send, recv_sem=recv,
            device_id={"dp": dev}, device_id_type=MESH,
        )

    barrier = pltpu.get_barrier_semaphore()
    partners = [*left.values(), *right.values(), sib]
    for dev in partners:
        pl.semaphore_signal(barrier, inc=1, device_id={"dp": dev}, device_id_type=MESH)

    width = wd.shape[0]
    pool, pairs = pl.ds(0, POOL), [pl.ds(2 * HD * p, 2 * HD) for p in range(2)]
    moves = {
        "k0": (kc_ref.at[:, pairs[0]], kb.at[pool, pairs[0]]),
        "q": (q_ref, q),
        "pt": (pt_in, pt),
        "cl": (cl_in, cl),
        "nk": (nk_ref, nk),
        "v0": (vc_ref.at[:, pairs[0]], vb.at[pool, pairs[0]]),
        "nv": (nv_ref, nv),
        "li": (li_ref, li),
        "gain": (gain_ref, gain),
        "k1": (kc_ref.at[:, pairs[1]], kb.at[pool, pairs[1]]),
        "v1": (vc_ref.at[:, pairs[1]], vb.at[pool, pairs[1]]),
        "bs": (bs_in, bs),
        "wg": (wg_ref, wgu.at[pl.ds(0, width)]),
        "wu": (wu_ref, wgu.at[pl.ds(width, width)]),
        "wd": (wd_ref, wd),
    }
    loads = {
        name: pltpu.make_async_copy(src, dst, lsem.at[i])
        for i, (name, (src, dst)) in enumerate(moves.items())
    }
    for name in list(moves)[:12]:
        loads[name].start()

    def lanes(j):
        return pl.ds(j * W, W)

    def sent_lanes(j):
        return pl.ds(j * W, W + SCALE if j == NJ - 1 else W)

    def ag(src, dst, j, dev):
        return remote(
            gath.at[0, src, :, sent_lanes(j)], gath.at[0, dst, :, sent_lanes(j)],
            ag_send.at[0], ag_recv.at[dst, j], dev,
        )

    groups = ((0, 1), (1, 4), (5, 4), (9, 4), (13, 3))

    def ag_sib(group, j):
        part = pl.ds(*groups[group])
        return remote(
            gath.at[0, part, :, sent_lanes(j)], gath.at[1, part, :, sent_lanes(j)],
            as_send.at[0], as_recv.at[group, j], sib,
        )

    def goes(m, j, sign):
        return m < 8 or (j < NJ // 2) == (sign > 0)

    def spread(m, j):
        for n in children(m):
            for sign, devices in ((1, right), (-1, left)):
                if goes(n, j, sign):
                    ag(slot_of(-sign * m), slot_of(-sign * n), j, devices[n - m]).start()

    def arrive(m, j):
        for sign in (1, -1):
            if goes(m, j, sign):
                ag(0, slot_of(-sign * m), j, right[1]).wait_recv()

    def stacked(ref, width):
        for s in range(4):
            rows[2 * s : 2 * s + 2, :width] = ref[s].astype(jnp.float32)
        return rows[:, :width]

    loads["pt"].wait()
    loads["cl"].wait()
    col1 = lax.broadcasted_iota(jnp.int32, (1, KEYS), 1)
    page = lax.shift_right_logical(col1, 5)
    off = jnp.bitwise_and(col1, 31)
    slot_bias = []
    for b in range(2):
        count = jnp.zeros((1, KEYS), jnp.int32)
        for i in range(16):
            count = jnp.where(page == pt[b, i], cl[b] - 32 * i, count)
        slot_bias.append(jnp.where(off < count, 0.0, masked))
    row8 = lax.broadcasted_iota(jnp.int32, (8, KEYS), 0)
    col8 = lax.broadcasted_iota(jnp.int32, (8, KEYS), 1) - POOL
    rowb = jnp.bitwise_and(row8, 1)
    bias = jnp.where(
        rowb == 0,
        jnp.broadcast_to(slot_bias[0], (8, KEYS)),
        jnp.broadcast_to(slot_bias[1], (8, KEYS)),
    )
    fresh = (
        (col8 >= 0)
        & (col8 < 8)
        & (jnp.bitwise_and(col8, 1) == rowb)
        & (lax.shift_right_arithmetic(col8, 1) <= lax.shift_right_logical(row8, 1))
    )
    bias = jnp.where(fresh, 0.0, bias)

    loads["q"].wait()
    qf = stacked(q, D)
    loads["nk"].wait()
    loads["nv"].wait()
    zeros8 = jnp.zeros((8, KVH * HD), jnp.float32)
    kb[pl.ds(POOL, 16)] = jnp.concatenate([stacked(nk, KVH * HD), zeros8], 0).astype(jnp.bfloat16)
    vb[pl.ds(POOL, 16)] = jnp.concatenate([stacked(nv, KVH * HD), zeros8], 0).astype(jnp.bfloat16)
    kb[pl.ds(POOL + 16, 112)] = jnp.zeros((112, KVH * HD), jnp.bfloat16)
    vb[pl.ds(POOL + 16, 112)] = jnp.zeros((112, KVH * HD), jnp.bfloat16)
    scale = 1.0 / jnp.sqrt(jnp.float32(HD))
    blank = jnp.zeros((64, HD), jnp.float32)
    squares = jnp.zeros((8, 1), jnp.float32)
    for pair in range(KVH // 2):
        both = [
            jnp.concatenate(
                [qf[:, (16 * pair + 8 * i + g) * HD : (16 * pair + 8 * i + g + 1) * HD] for g in range(8)], 0
            )
            for i in range(2)
        ]
        both = jnp.concatenate(
            [jnp.concatenate([both[0], blank], 1), jnp.concatenate([blank, both[1]], 1)], 0
        ).astype(jnp.bfloat16)
        place = slice(2 * pair * HD, 2 * (pair + 1) * HD)
        loads[("k0", "k1")[pair]].wait()
        scores = lax.dot_general(
            both, kb[:, place], (((1,), (1,)), ((), ())), preferred_element_type=jnp.float32
        )
        scores = (scores.reshape(16, 8, KEYS) * scale + bias[None]).reshape(128, KEYS)
        highest = jnp.max(scores, axis=-1, keepdims=True)
        expo = jnp.exp(scores - highest)
        total = jnp.sum(expo, axis=-1, keepdims=True)
        loads[("v0", "v1")[pair]].wait()
        mixed = jnp.dot(
            expo.astype(jnp.bfloat16), vb[:, place], preferred_element_type=jnp.float32
        ) / total
        attention = jnp.concatenate(
            [
                mixed[64 * i + 8 * g : 64 * i + 8 * g + 8, i * HD : (i + 1) * HD]
                for i in range(2)
                for g in range(8)
            ],
            1,
        ).astype(jnp.bfloat16).astype(jnp.float32)
        if pair == 0:
            loads["li"].wait()
            inputs = stacked(li, D)
            loads["gain"].wait()
        mine = slice(pair * D // 2, (pair + 1) * D // 2)
        residual = inputs[:, mine] + attention
        res[:, mine] = residual
        squares += jnp.sum(residual * residual, axis=-1, keepdims=True)
        row = residual * gain[:, mine]
        for c in range(NC // NJ):
            both = [row[:, (2 * c + fold) * CW : (2 * c + fold + 1) * CW] for fold in range(2)]
            start = pair * W + c * CW
            gath[0, 0, :, start : start + CW] = jnp.concatenate(both, 0).astype(jnp.bfloat16)
        if pair == 0:
            pl.semaphore_wait(barrier, len(partners))
        else:
            loads["bs"].wait()
            row_scale = jnp.broadcast_to(lax.rsqrt(squares / D + eps), (8, SCALE))
            live = jnp.bitwise_and(lax.broadcasted_iota(jnp.int32, (8, SCALE), 0), 1) < bs[0]
            row_scale = jnp.where(live, row_scale, 0.0)
            high = row_scale.astype(jnp.bfloat16).astype(jnp.float32)
            gath[0, 0, :, 2 * W :] = jnp.concatenate([high, row_scale - high], 0).astype(jnp.bfloat16)
        spread(0, pair)
        ag_sib(0, pair).start()
    for name in ("wg", "wu", "wd"):
        loads[name].start()

    def piece(c):
        return pl.ds(c * CW, CW)

    def features(c):
        return pl.ds(c * 2 * CW, 2 * CW)

    def gate_up(half, j):
        block = gath[:, pl.ds(half * 8, 8), :, lanes(j)].astype(jnp.float32)
        block = block.reshape(16, 2, 8, W)
        block = jnp.concatenate(
            [
                block[:, fold, :, c * CW : (c + 1) * CW].reshape(128, CW)
                for c in range(NC // NJ)
                for fold in range(2)
            ],
            1,
        )
        term = lax.dot_general(
            wgu[:, pl.ds(j * 2 * W, 2 * W)], block.astype(jnp.bfloat16),
            (((1,), (1,)), ((), ())), preferred_element_type=jnp.float32,
        )
        if j == 0:
            acc[half] = term
        else:
            acc[half] += term

    def activate(half):
        parts = gath[:, pl.ds(half * 8, 8), :, pl.ds(2 * W, SCALE)].astype(jnp.float32)
        parts = parts.reshape(16, 2, 8, SCALE)
        row_scale = (parts[:, 0] + parts[:, 1]).reshape(128, SCALE).T[:1]
        gate = acc[half, :width] * row_scale
        value = gate / (1.0 + jnp.exp(-gate)) * (acc[half, width:] * row_scale)
        hid[half] = value.T.astype(jnp.bfloat16)

    def sib_sum(half, c):
        slots = pl.ds(half * 8, 8)
        return remote(
            sibs.at[slots, :, piece(c)], sibr.at[slots, :, piece(c)],
            ss_send.at[0], ss_recv.at[half, c], sib,
        )

    def down(half):
        def step(c, carry):
            term = jnp.dot(hid[half], wd[:, features(c)], preferred_element_type=jnp.float32)
            both = [
                term[:, fold * CW : (fold + 1) * CW].reshape(2, 8, 1, 8, CW) for fold in range(2)
            ]
            both = jnp.concatenate(both, 2).reshape(2, 8, 16, CW)
            slots = pl.ds(half * 8, 8)
            sibs[slots, :, piece(c)] = both[1].astype(jnp.bfloat16)
            sib_sum(half, c).start()
            own[slots, :, piece(c)] = both[0]
            return carry

        lax.fori_loop(0, NC, step, 0)

    def plus(m, j):
        return remote(
            sp.at[m - 1, :, lanes(j)], rp.at[m - 1, :, lanes(j)],
            ps_send.at[m // 8], ps_recv.at[m - 1, j], right[m - PARENT[m]],
        )

    def minus(m, j):
        return remote(
            sm.at[m - 1, :, lanes(j)], rm.at[m - 1, :, lanes(j)],
            ms_send.at[m // 8], ms_recv.at[m - 1, j], left[m - PARENT[m]],
        )

    sides = ((1, plus, sp, rp), (-1, minus, sm, rm))

    def pass_on(m, j):
        for sign, copy, leaving, arrived in sides:
            if not goes(m, j, sign):
                continue
            slot = slot_of(sign * m)
            value = own[slot, :, lanes(j)] + sibr[slot, :, lanes(j)].astype(jnp.float32)
            for source in children(m):
                if goes(source, j, sign):
                    copy(source, j).wait_recv()
                    value = value + arrived[source - 1, :, lanes(j)].astype(jnp.float32)
            leaving[m - 1, :, lanes(j)] = value.astype(jnp.bfloat16)
            copy(m, j).start()

    def gathered(group):
        for j in range(NJ):
            ag_sib(group, j).wait_recv()

    for stage in range(1, 4):
        for j in range(NJ):
            arrive(2 * stage, j)
            spread(2 * stage, j)
        for j in range(NJ):
            arrive(2 * stage - 1, j)
            ag_sib(stage, j).start()

    for group in range(3):
        gathered(group)
    loads["wg"].wait()
    loads["wu"].wait()
    for j in range(NJ):
        gate_up(0, j)
    activate(0)
    loads["wd"].wait()
    down(0)

    for j in range(NJ):
        arrive(7, j)
        arrive(8, j)
        ag_sib(4, j).start()
    for c in range(NC):
        sib_sum(0, c).wait_recv()
    for j in range(NJ):
        pass_on(3, j)

    for j in range(NJ):
        for group in (3, 4):
            ag_sib(group, j).wait_recv()
        gate_up(1, j)
    activate(1)
    down(1)
    for j in range(NJ):
        pass_on(1, j)
    for j in range(NJ):
        for c in range(j * NC // NJ, (j + 1) * NC // NJ):
            sib_sum(1, c).wait_recv()
        for m in (8, 7):
            pass_on(m, j)
    for m in (5, 6, 4, 2):
        for j in range(NJ):
            pass_on(m, j)

    alive = jnp.bitwise_and(lax.broadcasted_iota(jnp.int32, (8, CW), 0), 1) < bs[0]
    for j in range(NJ):
        for m in children(0):
            plus(m, j).wait_recv()
            minus(m, j).wait_recv()
        for c in range(j * NC // NJ, (j + 1) * NC // NJ):
            value = own[0, :, piece(c)] + sibr[0, :, piece(c)].astype(jnp.float32)
            for m in children(0):
                for arrived in (rp, rm):
                    value = value + arrived[m - 1, :, piece(c)].astype(jnp.float32)
            for fold in range(2):
                place = pl.ds((2 * c + fold) * CW, CW)
                done = res[:, place] + value[8 * fold : 8 * fold + 8]
                out_ref[:, place] = jnp.where(alive, done, 0.0).astype(jnp.bfloat16)

    def sent(part, sem):
        remote(part, part, sem, sem, sib).wait_send()

    sent(gath.at[0, pl.ds(1, 15)], ag_send.at[0])
    sent(gath.at[0], as_send.at[0])
    sent(sibs, ss_send.at[0])
    sent(sp.at[7, :, pl.ds(0, HALF // 2)], ps_send.at[1])
    sent(sm.at[7, :, pl.ds(0, HALF // 2)], ms_send.at[1])
    sent(sp.at[pl.ds(0, 7)], ps_send.at[0])
    sent(sm.at[pl.ds(0, 7)], ms_send.at[0])


def local(
    layer_input, queries, new_keys, new_values, key_cache, value_cache, norm_gain,
    gate_weight, up_weight, down_weight, batch_sizes, cache_lengths, page_table,
):
    vmem = pl.BlockSpec(memory_space=pltpu.VMEM)
    hbm = pl.BlockSpec(memory_space=pltpu.HBM)
    width = down_weight.shape[0]
    bf16, f32 = jnp.bfloat16, jnp.float32
    dma = pltpu.SemaphoreType.DMA
    out = pl.pallas_call(
        kernel,
        out_shape=pltpu.VMEM((8, D), bf16),
        in_specs=[hbm] * 13,
        out_specs=vmem,
        scratch_shapes=[
            pltpu.SMEM((1,), jnp.int32),
            pltpu.SMEM((2,), jnp.int32),
            pltpu.SMEM((2, 16), jnp.int32),
            pltpu.VMEM((4, 2, D), bf16),
            pltpu.VMEM((4, 2, D), bf16),
            pltpu.VMEM((4, 2, KVH * HD), bf16),
            pltpu.VMEM((4, 2, KVH * HD), bf16),
            pltpu.VMEM((1, D), f32),
            pltpu.VMEM((KEYS, KVH * HD), bf16),
            pltpu.VMEM((KEYS, KVH * HD), bf16),
            pltpu.VMEM((2 * width, D), bf16),
            pltpu.VMEM((width, D), bf16),
            pltpu.VMEM((8, D), f32),
            pltpu.VMEM((8, D), f32),
            pltpu.VMEM((2, 16, 16, HALF + SCALE), bf16),
            pltpu.VMEM((2, 2 * width, 128), f32),
            pltpu.VMEM((2, 128, width), bf16),
            pltpu.VMEM((16, 16, HALF), f32),
            pltpu.VMEM((16, 16, HALF), bf16),
            pltpu.VMEM((16, 16, HALF), bf16),
            pltpu.VMEM((8, 16, HALF), bf16),
            pltpu.VMEM((8, 16, HALF), bf16),
            pltpu.VMEM((8, 16, HALF), bf16),
            pltpu.VMEM((8, 16, HALF), bf16),
            dma((15,)),
            dma((1,)),
            dma((16, NJ)),
            dma((1,)),
            dma((5, NJ)),
            dma((2,)),
            dma((8, NJ)),
            dma((2,)),
            dma((8, NJ)),
            dma((1,)),
            dma((2, NC)),
        ],
        compiler_params=pltpu.CompilerParams(
            collective_id=0, has_side_effects=True, vmem_limit_bytes=56 * 1024 * 1024
        ),
    )(
        batch_sizes,
        cache_lengths,
        page_table,
        layer_input,
        queries,
        new_keys,
        new_values,
        norm_gain.reshape(1, D),
        key_cache.reshape(POOL, KVH * HD),
        value_cache.reshape(POOL, KVH * HD),
        gate_weight.T,
        up_weight.T,
        down_weight,
    )
    return out.reshape(4, 2, D)


def solution(mesh):
    placed = (
        P(None, ("rep", "dp"), None),
        P(None, ("rep", "dp"), None),
        P(None, ("rep", "dp"), None),
        P(None, ("rep", "dp"), None),
        P(("rep", "dp"), None, None),
        P(("rep", "dp"), None, None),
        P(),
        P(None, "dp"),
        P(None, "dp"),
        P("dp", None),
        P(("rep", "dp")),
        P(("rep", "dp")),
        P(("rep", "dp"), None),
    )
    return jax.shard_map(
        local, mesh=mesh, in_specs=placed, out_specs=P(None, ("rep", "dp"), None), check_vma=False
    )
```

```python
import jax
import jax.numpy as jnp
from jax import lax
from jax.experimental import pallas as pl
from jax.experimental.pallas import tpu as pltpu
from jax.sharding import PartitionSpec as P

D = 4096
H = 32
KVH = 4
HD = 128
HALF = D // 2
NJ = 2
W = HALF // NJ
SCALE = 128
NC = 4
CW = HALF // NC
REPS = 16
POOL = 1024
KEYS = POOL + 128

PARENT = {1: 0, 2: 0, 3: 2, 4: 2, 5: 4, 6: 4, 7: 6, 8: 6}


def children(m):
    return [n for n in sorted(PARENT, reverse=True) if PARENT[n] == m]


masked = -1e30
eps = 1e-05
LOGICAL = pl.DeviceIdType.LOGICAL


def slot_of(offset):
    if offset == 8 or offset == -8:
        return 15
    return 2 * offset if offset >= 0 else -2 * offset - 1


def kernel(
    bs_in, cl_in, pt_in, li_ref, q_ref, nk_ref, nv_ref, gain_ref,
    kc_ref, vc_ref, wg_ref, wu_ref, wd_ref,
    out_ref,
    bs, cl, pt, li, q, nk, nv, gain, kb, vb, wgu, wd, rows, res, gath, acc, hid, own, sibs, sibr,
    sp, sm, rp, rm,
    lsem, ag_send, ag_recv, as_send, as_recv,
    ps_send, ps_recv, ms_send, ms_recv, ss_send, ss_recv,
):
    me, rep = lax.axis_index("dp"), lax.axis_index("rep")

    def place(dp):
        return dp * REPS + rep

    steps = sorted({n - m for n, m in PARENT.items()})
    right = {step: place(lax.rem(me + 2 * step, 32)) for step in steps}
    left = {step: place(lax.rem(me + 32 - 2 * step, 32)) for step in steps}
    sib = place(me + 1 - 2 * lax.rem(me, 2))

    def remote(src, dst, send, recv, dev):
        return pltpu.make_async_remote_copy(
            src_ref=src, dst_ref=dst, send_sem=send, recv_sem=recv,
            device_id=dev, device_id_type=LOGICAL,
        )

    barrier = pltpu.get_barrier_semaphore()
    partners = [*left.values(), *right.values(), sib]
    for dev in partners:
        pl.semaphore_signal(barrier, inc=1, device_id=dev, device_id_type=LOGICAL)

    width = wd.shape[0]
    pool, pairs = pl.ds(0, POOL), [pl.ds(2 * HD * p, 2 * HD) for p in range(2)]
    moves = {
        "k0": (kc_ref.at[:, pairs[0]], kb.at[pool, pairs[0]]),
        "q": (q_ref, q),
        "pt": (pt_in, pt),
        "cl": (cl_in, cl),
        "nk": (nk_ref, nk),
        "v0": (vc_ref.at[:, pairs[0]], vb.at[pool, pairs[0]]),
        "nv": (nv_ref, nv),
        "li": (li_ref, li),
        "gain": (gain_ref, gain),
        "k1": (kc_ref.at[:, pairs[1]], kb.at[pool, pairs[1]]),
        "v1": (vc_ref.at[:, pairs[1]], vb.at[pool, pairs[1]]),
        "bs": (bs_in, bs),
        "wg": (wg_ref, wgu.at[pl.ds(0, width)]),
        "wu": (wu_ref, wgu.at[pl.ds(width, width)]),
        "wd": (wd_ref, wd),
    }
    loads = {
        name: pltpu.make_async_copy(src, dst, lsem.at[i])
        for i, (name, (src, dst)) in enumerate(moves.items())
    }
    for load in loads.values():
        load.start()

    def lanes(j):
        return pl.ds(j * W, W)

    def sent_lanes(j):
        return pl.ds(j * W, W + SCALE if j == NJ - 1 else W)

    def ag(src, dst, j, dev):
        return remote(
            gath.at[0, src, :, sent_lanes(j)], gath.at[0, dst, :, sent_lanes(j)],
            ag_send.at[0], ag_recv.at[dst, j], dev,
        )

    groups = ((0, 1), (1, 4), (5, 4), (9, 4), (13, 3))

    def ag_sib(group, j):
        part = pl.ds(*groups[group])
        return remote(
            gath.at[0, part, :, sent_lanes(j)], gath.at[1, part, :, sent_lanes(j)],
            as_send.at[0], as_recv.at[group, j], sib,
        )

    def goes(m, j, sign):
        return m < 8 or (j < NJ // 2) == (sign > 0)

    def spread(m, j):
        for n in children(m):
            for sign, devices in ((1, right), (-1, left)):
                if goes(n, j, sign):
                    ag(slot_of(-sign * m), slot_of(-sign * n), j, devices[n - m]).start()

    def arrive(m, j):
        for sign in (1, -1):
            if goes(m, j, sign):
                ag(0, slot_of(-sign * m), j, right[1]).wait_recv()

    def stacked(ref, width):
        for s in range(4):
            rows[2 * s : 2 * s + 2, :width] = ref[s].astype(jnp.float32)
        return rows[:, :width]

    loads["pt"].wait()
    loads["cl"].wait()
    col1 = lax.broadcasted_iota(jnp.int32, (1, KEYS), 1)
    page = lax.shift_right_logical(col1, 5)
    off = jnp.bitwise_and(col1, 31)
    slot_bias = []
    for b in range(2):
        count = jnp.zeros((1, KEYS), jnp.int32)
        for i in range(16):
            count = jnp.where(page == pt[b, i], cl[b] - 32 * i, count)
        slot_bias.append(jnp.where(off < count, 0.0, masked))
    row8 = lax.broadcasted_iota(jnp.int32, (8, KEYS), 0)
    col8 = lax.broadcasted_iota(jnp.int32, (8, KEYS), 1) - POOL
    rowb = jnp.bitwise_and(row8, 1)
    bias = jnp.where(
        rowb == 0,
        jnp.broadcast_to(slot_bias[0], (8, KEYS)),
        jnp.broadcast_to(slot_bias[1], (8, KEYS)),
    )
    fresh = (
        (col8 >= 0)
        & (col8 < 8)
        & (jnp.bitwise_and(col8, 1) == rowb)
        & (lax.shift_right_arithmetic(col8, 1) <= lax.shift_right_logical(row8, 1))
    )
    bias = jnp.where(fresh, 0.0, bias)

    loads["q"].wait()
    qf = stacked(q, D)
    loads["nk"].wait()
    loads["nv"].wait()
    zeros8 = jnp.zeros((8, KVH * HD), jnp.float32)
    kb[pl.ds(POOL, 16)] = jnp.concatenate([stacked(nk, KVH * HD), zeros8], 0).astype(jnp.bfloat16)
    vb[pl.ds(POOL, 16)] = jnp.concatenate([stacked(nv, KVH * HD), zeros8], 0).astype(jnp.bfloat16)
    kb[pl.ds(POOL + 16, 112)] = jnp.zeros((112, KVH * HD), jnp.bfloat16)
    vb[pl.ds(POOL + 16, 112)] = jnp.zeros((112, KVH * HD), jnp.bfloat16)
    scale = 1.0 / jnp.sqrt(jnp.float32(HD))
    blank = jnp.zeros((64, HD), jnp.float32)
    squares = jnp.zeros((8, 1), jnp.float32)
    for pair in range(KVH // 2):
        both = [
            jnp.concatenate(
                [qf[:, (16 * pair + 8 * i + g) * HD : (16 * pair + 8 * i + g + 1) * HD] for g in range(8)], 0
            )
            for i in range(2)
        ]
        both = jnp.concatenate(
            [jnp.concatenate([both[0], blank], 1), jnp.concatenate([blank, both[1]], 1)], 0
        ).astype(jnp.bfloat16)
        these = slice(2 * pair * HD, 2 * (pair + 1) * HD)
        loads[("k0", "k1")[pair]].wait()
        scores = lax.dot_general(
            both, kb[:, these], (((1,), (1,)), ((), ())), preferred_element_type=jnp.float32
        )
        scores = (scores.reshape(16, 8, KEYS) * scale + bias[None]).reshape(128, KEYS)
        highest = jnp.max(scores, axis=-1, keepdims=True)
        expo = jnp.exp(scores - highest)
        total = jnp.sum(expo, axis=-1, keepdims=True)
        loads[("v0", "v1")[pair]].wait()
        mixed = jnp.dot(
            expo.astype(jnp.bfloat16), vb[:, these], preferred_element_type=jnp.float32
        ) / total
        attention = jnp.concatenate(
            [
                mixed[64 * i + 8 * g : 64 * i + 8 * g + 8, i * HD : (i + 1) * HD]
                for i in range(2)
                for g in range(8)
            ],
            1,
        ).astype(jnp.bfloat16).astype(jnp.float32)
        if pair == 0:
            loads["li"].wait()
            inputs = stacked(li, D)
            loads["gain"].wait()
        mine = slice(pair * D // 2, (pair + 1) * D // 2)
        residual = inputs[:, mine] + attention
        res[:, mine] = residual
        squares += jnp.sum(residual * residual, axis=-1, keepdims=True)
        row = residual * gain[:, mine]
        for c in range(NC // NJ):
            both = [row[:, (2 * c + fold) * CW : (2 * c + fold + 1) * CW] for fold in range(2)]
            start = pair * W + c * CW
            gath[0, 0, :, start : start + CW] = jnp.concatenate(both, 0).astype(jnp.bfloat16)
        if pair == 0:
            pl.semaphore_wait(barrier, len(partners))
        else:
            loads["bs"].wait()
            row_scale = jnp.broadcast_to(lax.rsqrt(squares / D + eps), (8, SCALE))
            live = jnp.bitwise_and(lax.broadcasted_iota(jnp.int32, (8, SCALE), 0), 1) < bs[0]
            row_scale = jnp.where(live, row_scale, 0.0)
            high = row_scale.astype(jnp.bfloat16).astype(jnp.float32)
            gath[0, 0, :, 2 * W :] = jnp.concatenate([high, row_scale - high], 0).astype(jnp.bfloat16)
        spread(0, pair)
        ag_sib(0, pair).start()
    def piece(c):
        return pl.ds(c * CW, CW)

    def features(c):
        return pl.ds(c * 2 * CW, 2 * CW)

    def gate_up(half, j):
        block = gath[:, pl.ds(half * 8, 8), :, lanes(j)].astype(jnp.float32)
        block = block.reshape(16, 2, 8, W)
        block = jnp.concatenate(
            [
                block[:, fold, :, c * CW : (c + 1) * CW].reshape(128, CW)
                for c in range(NC // NJ)
                for fold in range(2)
            ],
            1,
        )
        term = lax.dot_general(
            wgu[:, pl.ds(j * 2 * W, 2 * W)], block.astype(jnp.bfloat16),
            (((1,), (1,)), ((), ())), preferred_element_type=jnp.float32,
        )
        if j == 0:
            acc[half] = term
        else:
            acc[half] += term

    def activate(half):
        parts = gath[:, pl.ds(half * 8, 8), :, pl.ds(2 * W, SCALE)].astype(jnp.float32)
        parts = parts.reshape(16, 2, 8, SCALE)
        row_scale = (parts[:, 0] + parts[:, 1]).reshape(128, SCALE).T[:1]
        gate = acc[half, :width] * row_scale
        value = gate / (1.0 + jnp.exp(-gate)) * (acc[half, width:] * row_scale)
        hid[half] = value.T.astype(jnp.bfloat16)

    def sib_sum(half, c):
        slots = pl.ds(half * 8, 8)
        return remote(
            sibs.at[slots, :, piece(c)], sibr.at[slots, :, piece(c)],
            ss_send.at[0], ss_recv.at[half, c], sib,
        )

    def down(half):
        def step(c, carry):
            term = jnp.dot(hid[half], wd[:, features(c)], preferred_element_type=jnp.float32)
            both = [
                term[:, fold * CW : (fold + 1) * CW].reshape(2, 8, 1, 8, CW) for fold in range(2)
            ]
            both = jnp.concatenate(both, 2).reshape(2, 8, 16, CW)
            slots = pl.ds(half * 8, 8)
            sibs[slots, :, piece(c)] = both[1].astype(jnp.bfloat16)
            sib_sum(half, c).start()
            own[slots, :, piece(c)] = both[0]
            return carry

        lax.fori_loop(0, NC, step, 0)

    def plus(m, j):
        return remote(
            sp.at[m - 1, :, lanes(j)], rp.at[m - 1, :, lanes(j)],
            ps_send.at[m // 8], ps_recv.at[m - 1, j], right[m - PARENT[m]],
        )

    def minus(m, j):
        return remote(
            sm.at[m - 1, :, lanes(j)], rm.at[m - 1, :, lanes(j)],
            ms_send.at[m // 8], ms_recv.at[m - 1, j], left[m - PARENT[m]],
        )

    sides = ((1, plus, sp, rp), (-1, minus, sm, rm))

    def pass_on(m, j):
        for sign, copy, leaving, arrived in sides:
            if not goes(m, j, sign):
                continue
            slot = slot_of(sign * m)
            value = own[slot, :, lanes(j)] + sibr[slot, :, lanes(j)].astype(jnp.float32)
            for source in children(m):
                if goes(source, j, sign):
                    copy(source, j).wait_recv()
                    value = value + arrived[source - 1, :, lanes(j)].astype(jnp.float32)
            leaving[m - 1, :, lanes(j)] = value.astype(jnp.bfloat16)
            copy(m, j).start()

    def gathered(group):
        for j in range(NJ):
            ag_sib(group, j).wait_recv()

    for stage in range(1, 4):
        for j in range(NJ):
            arrive(2 * stage, j)
            spread(2 * stage, j)
        for j in range(NJ):
            arrive(2 * stage - 1, j)
            ag_sib(stage, j).start()

    for group in range(3):
        gathered(group)
    loads["wg"].wait()
    loads["wu"].wait()
    for j in range(NJ):
        gate_up(0, j)
    activate(0)
    loads["wd"].wait()
    down(0)

    for j in range(NJ):
        arrive(7, j)
        arrive(8, j)
        ag_sib(4, j).start()
    for c in range(NC):
        sib_sum(0, c).wait_recv()
    for j in range(NJ):
        pass_on(3, j)

    for j in range(NJ):
        for group in (3, 4):
            ag_sib(group, j).wait_recv()
        gate_up(1, j)
    activate(1)
    down(1)
    for j in range(NJ):
        pass_on(1, j)
    for j in range(NJ):
        for c in range(j * NC // NJ, (j + 1) * NC // NJ):
            sib_sum(1, c).wait_recv()
        for m in (8, 7):
            pass_on(m, j)
    for m in (5, 6, 4, 2):
        for j in range(NJ):
            pass_on(m, j)

    alive = jnp.bitwise_and(lax.broadcasted_iota(jnp.int32, (8, CW), 0), 1) < bs[0]
    for j in range(NJ):
        for m in children(0):
            plus(m, j).wait_recv()
            minus(m, j).wait_recv()
        for c in range(j * NC // NJ, (j + 1) * NC // NJ):
            value = own[0, :, piece(c)] + sibr[0, :, piece(c)].astype(jnp.float32)
            for m in children(0):
                for arrived in (rp, rm):
                    value = value + arrived[m - 1, :, piece(c)].astype(jnp.float32)
            for fold in range(2):
                place = pl.ds((2 * c + fold) * CW, CW)
                done = res[:, place] + value[8 * fold : 8 * fold + 8]
                out_ref[:, place] = jnp.where(alive, done, 0.0).astype(jnp.bfloat16)

    def sent(part, sem):
        remote(part, part, sem, sem, sib).wait_send()

    sent(gath.at[0, pl.ds(1, 15)], ag_send.at[0])
    sent(gath.at[0], as_send.at[0])
    sent(sibs, ss_send.at[0])
    sent(sp.at[7, :, pl.ds(0, HALF // 2)], ps_send.at[1])
    sent(sm.at[7, :, pl.ds(0, HALF // 2)], ms_send.at[1])
    sent(sp.at[pl.ds(0, 7)], ps_send.at[0])
    sent(sm.at[pl.ds(0, 7)], ms_send.at[0])


def local(
    layer_input, queries, new_keys, new_values, key_cache, value_cache, norm_gain,
    gate_weight, up_weight, down_weight, batch_sizes, cache_lengths, page_table,
):
    vmem = pl.BlockSpec(memory_space=pltpu.VMEM)
    hbm = pl.BlockSpec(memory_space=pltpu.HBM)
    width = down_weight.shape[0]
    bf16, f32 = jnp.bfloat16, jnp.float32
    dma = pltpu.SemaphoreType.DMA
    out = pl.pallas_call(
        kernel,
        out_shape=pltpu.VMEM((8, D), bf16),
        in_specs=[hbm] * 13,
        out_specs=vmem,
        scratch_shapes=[
            pltpu.SMEM((1,), jnp.int32),
            pltpu.SMEM((2,), jnp.int32),
            pltpu.SMEM((2, 16), jnp.int32),
            pltpu.VMEM((4, 2, D), bf16),
            pltpu.VMEM((4, 2, D), bf16),
            pltpu.VMEM((4, 2, KVH * HD), bf16),
            pltpu.VMEM((4, 2, KVH * HD), bf16),
            pltpu.VMEM((1, D), f32),
            pltpu.VMEM((KEYS, KVH * HD), bf16),
            pltpu.VMEM((KEYS, KVH * HD), bf16),
            pltpu.VMEM((2 * width, D), bf16),
            pltpu.VMEM((width, D), bf16),
            pltpu.VMEM((8, D), f32),
            pltpu.VMEM((8, D), f32),
            pltpu.VMEM((2, 16, 16, HALF + SCALE), bf16),
            pltpu.VMEM((2, 2 * width, 128), f32),
            pltpu.VMEM((2, 128, width), bf16),
            pltpu.VMEM((16, 16, HALF), f32),
            pltpu.VMEM((16, 16, HALF), bf16),
            pltpu.VMEM((16, 16, HALF), bf16),
            pltpu.VMEM((8, 16, HALF), bf16),
            pltpu.VMEM((8, 16, HALF), bf16),
            pltpu.VMEM((8, 16, HALF), bf16),
            pltpu.VMEM((8, 16, HALF), bf16),
            dma((15,)),
            dma((1,)),
            dma((16, NJ)),
            dma((1,)),
            dma((5, NJ)),
            dma((2,)),
            dma((8, NJ)),
            dma((2,)),
            dma((8, NJ)),
            dma((1,)),
            dma((2, NC)),
        ],
        compiler_params=pltpu.CompilerParams(
            collective_id=0, has_side_effects=True, vmem_limit_bytes=56 * 1024 * 1024
        ),
    )(
        batch_sizes,
        cache_lengths,
        page_table,
        layer_input,
        queries,
        new_keys,
        new_values,
        norm_gain.reshape(1, D),
        key_cache.reshape(POOL, KVH * HD),
        value_cache.reshape(POOL, KVH * HD),
        gate_weight.T,
        up_weight.T,
        down_weight,
    )
    return out.reshape(4, 2, D)


def solution(mesh):
    placed = (
        P(None, ("rep", "dp"), None),
        P(None, ("rep", "dp"), None),
        P(None, ("rep", "dp"), None),
        P(None, ("rep", "dp"), None),
        P(("rep", "dp"), None, None),
        P(("rep", "dp"), None, None),
        P(),
        P(None, "dp"),
        P(None, "dp"),
        P("dp", None),
        P(("rep", "dp")),
        P(("rep", "dp")),
        P(("rep", "dp"), None),
    )
    return jax.shard_map(
        local, mesh=mesh, in_specs=placed, out_specs=P(None, ("rep", "dp"), None), check_vma=False
    )
```

```python
import jax
import jax.numpy as jnp
from jax import lax
from jax.experimental import pallas as pl
from jax.experimental.pallas import tpu as pltpu
from jax.sharding import PartitionSpec as P

D = 4096
H = 32
KVH = 4
HD = 128
HALF = D // 2
NJ = 2
W = HALF // NJ
SCALE = 128
NC = 4
CW = HALF // NC
REPS = 16
POOL = 1024
KEYS = POOL + 128

PARENT = {1: 0, 2: 0, 3: 2, 4: 2, 5: 4, 6: 4, 7: 6, 8: 6}


def children(m):
    return [n for n in sorted(PARENT, reverse=True) if PARENT[n] == m]


masked = -1e30
eps = 1e-05
LOGICAL = pl.DeviceIdType.LOGICAL


def slot_of(offset):
    if offset == 8 or offset == -8:
        return 15
    return 2 * offset if offset >= 0 else -2 * offset - 1


def kernel(
    bs_in, cl_in, pt_in, li_ref, q_ref, nk_ref, nv_ref, gain_ref,
    kc_ref, vc_ref, wg_ref, wu_ref, wd_ref,
    out_ref,
    bs, cl, pt, li, q, nk, nv, gain, kb, vb, wgu, wd, rows, res, gath, acc, hid, own,
    sp, sm, rp, rm,
    lsem, w_send, w_recv, ag_send, ag_recv, ps_send, ps_recv, ms_send, ms_recv,
):
    me, rep = lax.axis_index("dp"), lax.axis_index("rep")

    def place(dp):
        return dp * REPS + rep

    steps = sorted({n - m for n, m in PARENT.items()})
    right = {step: place(lax.rem(me + 2 * step, 32)) for step in steps}
    left = {step: place(lax.rem(me + 32 - 2 * step, 32)) for step in steps}
    sib = place(me + 1 - 2 * lax.rem(me, 2))

    def remote(src, dst, send, recv, dev):
        return pltpu.make_async_remote_copy(
            src_ref=src, dst_ref=dst, send_sem=send, recv_sem=recv,
            device_id=dev, device_id_type=LOGICAL,
        )

    barrier = pltpu.get_barrier_semaphore()
    partners = [*left.values(), *right.values(), sib]
    for dev in partners:
        pl.semaphore_signal(barrier, inc=1, device_id=dev, device_id_type=LOGICAL)

    width = wd.shape[0] // 2
    pool, pairs = pl.ds(0, POOL), [pl.ds(2 * HD * p, 2 * HD) for p in range(2)]
    moves = {
        "k0": (kc_ref.at[:, pairs[0]], kb.at[pool, pairs[0]]),
        "q": (q_ref, q),
        "pt": (pt_in, pt),
        "cl": (cl_in, cl),
        "nk": (nk_ref, nk),
        "v0": (vc_ref.at[:, pairs[0]], vb.at[pool, pairs[0]]),
        "nv": (nv_ref, nv),
        "li": (li_ref, li),
        "gain": (gain_ref, gain),
        "k1": (kc_ref.at[:, pairs[1]], kb.at[pool, pairs[1]]),
        "v1": (vc_ref.at[:, pairs[1]], vb.at[pool, pairs[1]]),
        "bs": (bs_in, bs),
        "wg": (wg_ref, wgu.at[pl.ds(0, width)]),
        "wu": (wu_ref, wgu.at[pl.ds(width, width)]),
        "wd": (wd_ref, wd.at[pl.ds(0, width)]),
    }
    loads = {
        name: pltpu.make_async_copy(src, dst, lsem.at[i])
        for i, (name, (src, dst)) in enumerate(moves.items())
    }
    for load in loads.values():
        load.start()

    pl.semaphore_wait(barrier, len(partners))
    pushes = []
    for part in range(2):
        columns = pl.ds(part * D // 2, D // 2)
        for k, (src, full) in enumerate(((wg_ref, wgu), (wu_ref, wgu), (wd_ref, wd))):
            dst = full.at[pl.ds((2 + k) * width if k < 2 else width, width), columns]
            pushes.append((src.at[:, columns], dst))
    order = (0, 1, 3, 4, 2, 5)
    pushes = [
        remote(*pushes[k], w_send.at[i], w_recv.at[i], sib) for i, k in enumerate(order)
    ]
    for push in pushes:
        push.start()

    def lanes(j):
        return pl.ds(j * W, W)

    def sent_lanes(j):
        return pl.ds(j * W, W + SCALE if j == NJ - 1 else W)

    def ag(src, dst, j, dev):
        return remote(
            gath.at[src, :, sent_lanes(j)], gath.at[dst, :, sent_lanes(j)],
            ag_send.at[0], ag_recv.at[dst, j], dev,
        )

    def goes(m, j, sign):
        return m < 8 or (j < NJ // 2) == (sign > 0)

    def spread(m, j):
        for n in children(m):
            for sign, devices in ((1, right), (-1, left)):
                if goes(n, j, sign):
                    ag(slot_of(-sign * m), slot_of(-sign * n), j, devices[n - m]).start()

    def arrive(m, j):
        for sign in (1, -1):
            if goes(m, j, sign):
                ag(0, slot_of(-sign * m), j, right[1]).wait_recv()

    def stacked(ref, width):
        for s in range(4):
            rows[2 * s : 2 * s + 2, :width] = ref[s].astype(jnp.float32)
        return rows[:, :width]

    loads["pt"].wait()
    loads["cl"].wait()
    col1 = lax.broadcasted_iota(jnp.int32, (1, KEYS), 1)
    page = lax.shift_right_logical(col1, 5)
    off = jnp.bitwise_and(col1, 31)
    slot_bias = []
    for b in range(2):
        count = jnp.zeros((1, KEYS), jnp.int32)
        for i in range(16):
            count = jnp.where(page == pt[b, i], cl[b] - 32 * i, count)
        slot_bias.append(jnp.where(off < count, 0.0, masked))
    row8 = lax.broadcasted_iota(jnp.int32, (8, KEYS), 0)
    col8 = lax.broadcasted_iota(jnp.int32, (8, KEYS), 1) - POOL
    rowb = jnp.bitwise_and(row8, 1)
    bias = jnp.where(
        rowb == 0,
        jnp.broadcast_to(slot_bias[0], (8, KEYS)),
        jnp.broadcast_to(slot_bias[1], (8, KEYS)),
    )
    fresh = (
        (col8 >= 0)
        & (col8 < 8)
        & (jnp.bitwise_and(col8, 1) == rowb)
        & (lax.shift_right_arithmetic(col8, 1) <= lax.shift_right_logical(row8, 1))
    )
    bias = jnp.where(fresh, 0.0, bias)

    loads["q"].wait()
    qf = stacked(q, D)
    loads["nk"].wait()
    loads["nv"].wait()
    zeros8 = jnp.zeros((8, KVH * HD), jnp.float32)
    kb[pl.ds(POOL, 16)] = jnp.concatenate([stacked(nk, KVH * HD), zeros8], 0).astype(jnp.bfloat16)
    vb[pl.ds(POOL, 16)] = jnp.concatenate([stacked(nv, KVH * HD), zeros8], 0).astype(jnp.bfloat16)
    kb[pl.ds(POOL + 16, 112)] = jnp.zeros((112, KVH * HD), jnp.bfloat16)
    vb[pl.ds(POOL + 16, 112)] = jnp.zeros((112, KVH * HD), jnp.bfloat16)
    scale = 1.0 / jnp.sqrt(jnp.float32(HD))
    blank = jnp.zeros((64, HD), jnp.float32)
    squares = jnp.zeros((8, 1), jnp.float32)
    for pair in range(KVH // 2):
        both = [
            jnp.concatenate(
                [qf[:, (16 * pair + 8 * i + g) * HD : (16 * pair + 8 * i + g + 1) * HD] for g in range(8)], 0
            )
            for i in range(2)
        ]
        both = jnp.concatenate(
            [jnp.concatenate([both[0], blank], 1), jnp.concatenate([blank, both[1]], 1)], 0
        ).astype(jnp.bfloat16)
        these = slice(2 * pair * HD, 2 * (pair + 1) * HD)
        loads[("k0", "k1")[pair]].wait()
        scores = lax.dot_general(
            both, kb[:, these], (((1,), (1,)), ((), ())), preferred_element_type=jnp.float32
        )
        scores = (scores.reshape(16, 8, KEYS) * scale + bias[None]).reshape(128, KEYS)
        highest = jnp.max(scores, axis=-1, keepdims=True)
        expo = jnp.exp(scores - highest)
        total = jnp.sum(expo, axis=-1, keepdims=True)
        loads[("v0", "v1")[pair]].wait()
        mixed = jnp.dot(
            expo.astype(jnp.bfloat16), vb[:, these], preferred_element_type=jnp.float32
        ) / total
        attention = jnp.concatenate(
            [
                mixed[64 * i + 8 * g : 64 * i + 8 * g + 8, i * HD : (i + 1) * HD]
                for i in range(2)
                for g in range(8)
            ],
            1,
        ).astype(jnp.bfloat16).astype(jnp.float32)
        if pair == 0:
            loads["li"].wait()
            inputs = stacked(li, D)
            loads["gain"].wait()
        mine = slice(pair * D // 2, (pair + 1) * D // 2)
        residual = inputs[:, mine] + attention
        res[:, mine] = residual
        squares += jnp.sum(residual * residual, axis=-1, keepdims=True)
        row = residual * gain[:, mine]
        for c in range(NC // NJ):
            both = [row[:, (2 * c + fold) * CW : (2 * c + fold + 1) * CW] for fold in range(2)]
            start = pair * W + c * CW
            gath[0, :, start : start + CW] = jnp.concatenate(both, 0).astype(jnp.bfloat16)
        if pair == 1:
            loads["bs"].wait()
            row_scale = jnp.broadcast_to(lax.rsqrt(squares / D + eps), (8, SCALE))
            live = jnp.bitwise_and(lax.broadcasted_iota(jnp.int32, (8, SCALE), 0), 1) < bs[0]
            row_scale = jnp.where(live, row_scale, 0.0)
            high = row_scale.astype(jnp.bfloat16).astype(jnp.float32)
            gath[0, :, 2 * W :] = jnp.concatenate([high, row_scale - high], 0).astype(jnp.bfloat16)
        spread(0, pair)
    def piece(c):
        return pl.ds(c * CW, CW)

    def features(c):
        return pl.ds(c * 2 * CW, 2 * CW)

    def gate_up(j):
        block = gath[:, :, lanes(j)].astype(jnp.float32).reshape(16, 2, 8, W)
        block = jnp.concatenate(
            [
                block[:, fold, :, c * CW : (c + 1) * CW].reshape(128, CW)
                for c in range(NC // NJ)
                for fold in range(2)
            ],
            1,
        )
        term = lax.dot_general(
            wgu[:, pl.ds(j * 2 * W, 2 * W)], block.astype(jnp.bfloat16),
            (((1,), (1,)), ((), ())), preferred_element_type=jnp.float32,
        )
        if j == 0:
            acc[...] = term
        else:
            acc[...] += term

    def activate():
        parts = gath[:, :, pl.ds(2 * W, SCALE)].astype(jnp.float32).reshape(16, 2, 8, SCALE)
        row_scale = (parts[:, 0] + parts[:, 1]).reshape(128, SCALE).T[:1]
        for core in range(2):
            gate = acc[2 * core * width : (2 * core + 1) * width] * row_scale
            upward = acc[(2 * core + 1) * width : (2 * core + 2) * width] * row_scale
            value = gate / (1.0 + jnp.exp(-gate)) * upward
            hid[core] = value.T.astype(jnp.bfloat16)

    def down(c):
        term = sum(
            jnp.dot(
                hid[core], wd[pl.ds(core * width, width), features(c)],
                preferred_element_type=jnp.float32,
            )
            for core in range(2)
        )
        both = [term[:, fold * CW : (fold + 1) * CW].reshape(16, 1, 8, CW) for fold in range(2)]
        own[:, :, piece(c)] = jnp.concatenate(both, 1).reshape(16, 16, CW)

    def plus(m, j):
        return remote(
            sp.at[m - 1, :, lanes(j)], rp.at[m - 1, :, lanes(j)],
            ps_send.at[m // 8], ps_recv.at[m - 1, j], right[m - PARENT[m]],
        )

    def minus(m, j):
        return remote(
            sm.at[m - 1, :, lanes(j)], rm.at[m - 1, :, lanes(j)],
            ms_send.at[m // 8], ms_recv.at[m - 1, j], left[m - PARENT[m]],
        )

    sides = ((1, plus, sp, rp), (-1, minus, sm, rm))

    def pass_on(m, j):
        for sign, copy, leaving, arrived in sides:
            if not goes(m, j, sign):
                continue
            slot = slot_of(sign * m)
            value = own[slot, :, lanes(j)]
            for source in children(m):
                if goes(source, j, sign):
                    copy(source, j).wait_recv()
                    value = value + arrived[source - 1, :, lanes(j)].astype(jnp.float32)
            leaving[m - 1, :, lanes(j)] = value.astype(jnp.bfloat16)
            copy(m, j).start()

    for m in (2, 1, 4, 3, 6, 5):
        for j in range(NJ):
            arrive(m, j)
            spread(m, j)
    for name in ("wg", "wu"):
        loads[name].wait()
    for j in range(NJ):
        arrive(7, j)
        arrive(8, j)
        for push in pushes[2 * j : 2 * j + 2]:
            push.wait_recv()
        gate_up(j)
    activate()
    loads["wd"].wait()
    for j in range(NJ):
        pushes[4 + j].wait_recv()
        for c in range(j * NC // NJ, (j + 1) * NC // NJ):
            down(c)
        for m in (8, 7):
            pass_on(m, j)
    for m in (5, 6, 3, 4, 1, 2):
        for j in range(NJ):
            pass_on(m, j)

    alive = jnp.bitwise_and(lax.broadcasted_iota(jnp.int32, (8, CW), 0), 1) < bs[0]
    for j in range(NJ):
        for m in children(0):
            plus(m, j).wait_recv()
            minus(m, j).wait_recv()
        for c in range(j * NC // NJ, (j + 1) * NC // NJ):
            value = own[0, :, piece(c)]
            for m in children(0):
                for arrived in (rp, rm):
                    value = value + arrived[m - 1, :, piece(c)].astype(jnp.float32)
            for fold in range(2):
                place = pl.ds((2 * c + fold) * CW, CW)
                done = res[:, place] + value[8 * fold : 8 * fold + 8]
                out_ref[:, place] = jnp.where(alive, done, 0.0).astype(jnp.bfloat16)

    def sent(part, sem):
        remote(part, part, sem, sem, sib).wait_send()

    for push in pushes:
        push.wait_send()
    sent(gath.at[pl.ds(1, 15)], ag_send.at[0])
    sent(sp.at[7, :, pl.ds(0, HALF // 2)], ps_send.at[1])
    sent(sm.at[7, :, pl.ds(0, HALF // 2)], ms_send.at[1])
    sent(sp.at[pl.ds(0, 7)], ps_send.at[0])
    sent(sm.at[pl.ds(0, 7)], ms_send.at[0])


def local(
    layer_input, queries, new_keys, new_values, key_cache, value_cache, norm_gain,
    gate_weight, up_weight, down_weight, batch_sizes, cache_lengths, page_table,
):
    vmem = pl.BlockSpec(memory_space=pltpu.VMEM)
    hbm = pl.BlockSpec(memory_space=pltpu.HBM)
    width = down_weight.shape[0]
    bf16, f32 = jnp.bfloat16, jnp.float32
    dma = pltpu.SemaphoreType.DMA
    out = pl.pallas_call(
        kernel,
        out_shape=pltpu.VMEM((8, D), bf16),
        in_specs=[hbm] * 13,
        out_specs=vmem,
        scratch_shapes=[
            pltpu.SMEM((1,), jnp.int32),
            pltpu.SMEM((2,), jnp.int32),
            pltpu.SMEM((2, 16), jnp.int32),
            pltpu.VMEM((4, 2, D), bf16),
            pltpu.VMEM((4, 2, D), bf16),
            pltpu.VMEM((4, 2, KVH * HD), bf16),
            pltpu.VMEM((4, 2, KVH * HD), bf16),
            pltpu.VMEM((1, D), f32),
            pltpu.VMEM((KEYS, KVH * HD), bf16),
            pltpu.VMEM((KEYS, KVH * HD), bf16),
            pltpu.VMEM((4 * width, D), bf16),
            pltpu.VMEM((2 * width, D), bf16),
            pltpu.VMEM((8, D), f32),
            pltpu.VMEM((8, D), f32),
            pltpu.VMEM((16, 16, HALF + SCALE), bf16),
            pltpu.VMEM((4 * width, 128), f32),
            pltpu.VMEM((2, 128, width), bf16),
            pltpu.VMEM((16, 16, HALF), f32),
            pltpu.VMEM((8, 16, HALF), bf16),
            pltpu.VMEM((8, 16, HALF), bf16),
            pltpu.VMEM((8, 16, HALF), bf16),
            pltpu.VMEM((8, 16, HALF), bf16),
            dma((15,)),
            dma((6,)),
            dma((6,)),
            dma((1,)),
            dma((16, NJ)),
            dma((2,)),
            dma((8, NJ)),
            dma((2,)),
            dma((8, NJ)),
        ],
        compiler_params=pltpu.CompilerParams(
            collective_id=0, has_side_effects=True, vmem_limit_bytes=56 * 1024 * 1024
        ),
    )(
        batch_sizes,
        cache_lengths,
        page_table,
        layer_input,
        queries,
        new_keys,
        new_values,
        norm_gain.reshape(1, D),
        key_cache.reshape(POOL, KVH * HD),
        value_cache.reshape(POOL, KVH * HD),
        gate_weight.T,
        up_weight.T,
        down_weight,
    )
    return out.reshape(4, 2, D)


def solution(mesh):
    placed = (
        P(None, ("rep", "dp"), None),
        P(None, ("rep", "dp"), None),
        P(None, ("rep", "dp"), None),
        P(None, ("rep", "dp"), None),
        P(("rep", "dp"), None, None),
        P(("rep", "dp"), None, None),
        P(),
        P(None, "dp"),
        P(None, "dp"),
        P("dp", None),
        P(("rep", "dp")),
        P(("rep", "dp")),
        P(("rep", "dp"), None),
    )
    return jax.shard_map(
        local, mesh=mesh, in_specs=placed, out_specs=P(None, ("rep", "dp"), None), check_vma=False
    )
```

```python
import jax
import jax.numpy as jnp
from jax import lax
from jax.experimental import pallas as pl
from jax.experimental.pallas import tpu as pltpu
from jax.sharding import PartitionSpec as P

D = 4096
H = 32
KVH = 4
HD = 128
HALF = D // 2
NJ = 4
W = HALF // NJ
SCALE = 128
NC = 4
CW = HALF // NC
REPS = 16
POOL = 1024
KEYS = POOL + 128

PARENT = {1: 0, 2: 0, 3: 2, 4: 2, 5: 4, 6: 4, 7: 6, 8: 6}


def children(m):
    return [n for n in sorted(PARENT, reverse=True) if PARENT[n] == m]


masked = -1e30
eps = 1e-05
LOGICAL = pl.DeviceIdType.LOGICAL


def slot_of(offset):
    if offset == 8 or offset == -8:
        return 15
    return 2 * offset if offset >= 0 else -2 * offset - 1


def kernel(
    bs_in, cl_in, pt_in, li_ref, q_ref, nk_ref, nv_ref, gain_ref,
    kc_ref, vc_ref, wg_ref, wu_ref, wd_ref,
    out_ref,
    bs, cl, pt, li, q, nk, nv, gain, kb, vb, wgu, wd, rows, res, gath, acc, hid, own,
    sp, sm, rp, rm,
    lsem, w_send, w_recv, ag_send, ag_recv, ps_send, ps_recv, ms_send, ms_recv,
):
    me, rep = lax.axis_index("dp"), lax.axis_index("rep")

    def place(dp):
        return dp * REPS + rep

    steps = sorted({n - m for n, m in PARENT.items()})
    right = {step: place(lax.rem(me + 2 * step, 32)) for step in steps}
    left = {step: place(lax.rem(me + 32 - 2 * step, 32)) for step in steps}
    sib = place(me + 1 - 2 * lax.rem(me, 2))

    def remote(src, dst, send, recv, dev):
        return pltpu.make_async_remote_copy(
            src_ref=src, dst_ref=dst, send_sem=send, recv_sem=recv,
            device_id=dev, device_id_type=LOGICAL,
        )

    barrier = pltpu.get_barrier_semaphore()
    partners = [*left.values(), *right.values(), sib]
    for dev in partners:
        pl.semaphore_signal(barrier, inc=1, device_id=dev, device_id_type=LOGICAL)

    width = wd.shape[0] // 2
    pool, pairs = pl.ds(0, POOL), [pl.ds(2 * HD * p, 2 * HD) for p in range(2)]
    moves = {
        "k0": (kc_ref.at[:, pairs[0]], kb.at[pool, pairs[0]]),
        "q": (q_ref, q),
        "pt": (pt_in, pt),
        "cl": (cl_in, cl),
        "nk": (nk_ref, nk),
        "v0": (vc_ref.at[:, pairs[0]], vb.at[pool, pairs[0]]),
        "nv": (nv_ref, nv),
        "li": (li_ref, li),
        "gain": (gain_ref, gain),
        "k1": (kc_ref.at[:, pairs[1]], kb.at[pool, pairs[1]]),
        "v1": (vc_ref.at[:, pairs[1]], vb.at[pool, pairs[1]]),
        "bs": (bs_in, bs),
        "wg": (wg_ref, wgu.at[pl.ds(0, width)]),
        "wu": (wu_ref, wgu.at[pl.ds(width, width)]),
        "wd": (wd_ref, wd.at[pl.ds(0, width)]),
    }
    loads = {
        name: pltpu.make_async_copy(src, dst, lsem.at[i])
        for i, (name, (src, dst)) in enumerate(moves.items())
    }
    for load in loads.values():
        load.start()

    pl.semaphore_wait(barrier, len(partners))
    pushes = []
    for part in range(2):
        columns = pl.ds(part * D // 2, D // 2)
        for k, (src, full) in enumerate(((wg_ref, wgu), (wu_ref, wgu), (wd_ref, wd))):
            dst = full.at[pl.ds((2 + k) * width if k < 2 else width, width), columns]
            pushes.append((src.at[:, columns], dst))
    order = (0, 1, 3, 4, 2, 5)
    pushes = [
        remote(*pushes[k], w_send.at[i], w_recv.at[i], sib) for i, k in enumerate(order)
    ]
    for push in pushes:
        push.start()

    def lanes(j):
        return pl.ds(j * W, W)

    def sent_lanes(j):
        return pl.ds(j * W, W + SCALE if j == NJ - 1 else W)

    def ag(src, dst, j, dev):
        return remote(
            gath.at[src, :, sent_lanes(j)], gath.at[dst, :, sent_lanes(j)],
            ag_send.at[0], ag_recv.at[dst, j], dev,
        )

    def chunks(h):
        return range(h * NJ // 2, (h + 1) * NJ // 2)

    def goes(m, j, sign):
        return m < 8 or (j < NJ // 2) == (sign > 0)

    def spread(m, j):
        for n in children(m):
            for sign, devices in ((1, right), (-1, left)):
                if goes(n, j, sign):
                    ag(slot_of(-sign * m), slot_of(-sign * n), j, devices[n - m]).start()

    def arrive(m, j):
        for sign in (1, -1):
            if goes(m, j, sign):
                ag(0, slot_of(-sign * m), j, right[1]).wait_recv()

    def stacked(ref, width):
        for s in range(4):
            rows[2 * s : 2 * s + 2, :width] = ref[s].astype(jnp.float32)
        return rows[:, :width]

    loads["pt"].wait()
    loads["cl"].wait()
    col1 = lax.broadcasted_iota(jnp.int32, (1, KEYS), 1)
    page = lax.shift_right_logical(col1, 5)
    off = jnp.bitwise_and(col1, 31)
    slot_bias = []
    for b in range(2):
        count = jnp.zeros((1, KEYS), jnp.int32)
        for i in range(16):
            count = jnp.where(page == pt[b, i], cl[b] - 32 * i, count)
        slot_bias.append(jnp.where(off < count, 0.0, masked))
    row8 = lax.broadcasted_iota(jnp.int32, (8, KEYS), 0)
    col8 = lax.broadcasted_iota(jnp.int32, (8, KEYS), 1) - POOL
    rowb = jnp.bitwise_and(row8, 1)
    bias = jnp.where(
        rowb == 0,
        jnp.broadcast_to(slot_bias[0], (8, KEYS)),
        jnp.broadcast_to(slot_bias[1], (8, KEYS)),
    )
    fresh = (
        (col8 >= 0)
        & (col8 < 8)
        & (jnp.bitwise_and(col8, 1) == rowb)
        & (lax.shift_right_arithmetic(col8, 1) <= lax.shift_right_logical(row8, 1))
    )
    bias = jnp.where(fresh, 0.0, bias)

    loads["q"].wait()
    qf = stacked(q, D)
    loads["nk"].wait()
    loads["nv"].wait()
    zeros8 = jnp.zeros((8, KVH * HD), jnp.float32)
    kb[pl.ds(POOL, 16)] = jnp.concatenate([stacked(nk, KVH * HD), zeros8], 0).astype(jnp.bfloat16)
    vb[pl.ds(POOL, 16)] = jnp.concatenate([stacked(nv, KVH * HD), zeros8], 0).astype(jnp.bfloat16)
    kb[pl.ds(POOL + 16, 112)] = jnp.zeros((112, KVH * HD), jnp.bfloat16)
    vb[pl.ds(POOL + 16, 112)] = jnp.zeros((112, KVH * HD), jnp.bfloat16)
    scale = 1.0 / jnp.sqrt(jnp.float32(HD))
    blank = jnp.zeros((64, HD), jnp.float32)
    squares = jnp.zeros((8, 1), jnp.float32)
    for pair in range(KVH // 2):
        both = [
            jnp.concatenate(
                [qf[:, (16 * pair + 8 * i + g) * HD : (16 * pair + 8 * i + g + 1) * HD] for g in range(8)], 0
            )
            for i in range(2)
        ]
        both = jnp.concatenate(
            [jnp.concatenate([both[0], blank], 1), jnp.concatenate([blank, both[1]], 1)], 0
        ).astype(jnp.bfloat16)
        these = slice(2 * pair * HD, 2 * (pair + 1) * HD)
        loads[("k0", "k1")[pair]].wait()
        scores = lax.dot_general(
            both, kb[:, these], (((1,), (1,)), ((), ())), preferred_element_type=jnp.float32
        )
        scores = (scores.reshape(16, 8, KEYS) * scale + bias[None]).reshape(128, KEYS)
        highest = jnp.max(scores, axis=-1, keepdims=True)
        expo = jnp.exp(scores - highest)
        total = jnp.sum(expo, axis=-1, keepdims=True)
        loads[("v0", "v1")[pair]].wait()
        mixed = jnp.dot(
            expo.astype(jnp.bfloat16), vb[:, these], preferred_element_type=jnp.float32
        ) / total
        attention = jnp.concatenate(
            [
                mixed[64 * i + 8 * g : 64 * i + 8 * g + 8, i * HD : (i + 1) * HD]
                for i in range(2)
                for g in range(8)
            ],
            1,
        ).astype(jnp.bfloat16).astype(jnp.float32)
        if pair == 0:
            loads["li"].wait()
            inputs = stacked(li, D)
            loads["gain"].wait()
        mine = slice(pair * D // 2, (pair + 1) * D // 2)
        residual = inputs[:, mine] + attention
        res[:, mine] = residual
        squares += jnp.sum(residual * residual, axis=-1, keepdims=True)
        row = residual * gain[:, mine]
        for c in range(NC // 2):
            both = [row[:, (2 * c + fold) * CW : (2 * c + fold + 1) * CW] for fold in range(2)]
            start = pair * HALF // 2 + c * CW
            gath[0, :, start : start + CW] = jnp.concatenate(both, 0).astype(jnp.bfloat16)
        if pair == 1:
            loads["bs"].wait()
            row_scale = jnp.broadcast_to(lax.rsqrt(squares / D + eps), (8, SCALE))
            live = jnp.bitwise_and(lax.broadcasted_iota(jnp.int32, (8, SCALE), 0), 1) < bs[0]
            row_scale = jnp.where(live, row_scale, 0.0)
            high = row_scale.astype(jnp.bfloat16).astype(jnp.float32)
            gath[0, :, HALF:] = jnp.concatenate([high, row_scale - high], 0).astype(jnp.bfloat16)
        for j in chunks(pair):
            spread(0, j)
    def piece(c):
        return pl.ds(c * CW, CW)

    def features(c):
        return pl.ds(c * 2 * CW, 2 * CW)

    def gate_up(h):
        block = gath[:, :, pl.ds(h * HALF // 2, HALF // 2)].astype(jnp.float32)
        block = block.reshape(16, 2, 8, HALF // 2)
        block = jnp.concatenate(
            [
                block[:, fold, :, c * CW : (c + 1) * CW].reshape(128, CW)
                for c in range(NC // 2)
                for fold in range(2)
            ],
            1,
        )
        term = lax.dot_general(
            wgu[:, pl.ds(h * D // 2, D // 2)], block.astype(jnp.bfloat16),
            (((1,), (1,)), ((), ())), preferred_element_type=jnp.float32,
        )
        if h == 0:
            acc[...] = term
        else:
            acc[...] += term

    def activate():
        parts = gath[:, :, pl.ds(HALF, SCALE)].astype(jnp.float32).reshape(16, 2, 8, SCALE)
        row_scale = (parts[:, 0] + parts[:, 1]).reshape(128, SCALE).T[:1]
        for core in range(2):
            gate = acc[2 * core * width : (2 * core + 1) * width] * row_scale
            upward = acc[(2 * core + 1) * width : (2 * core + 2) * width] * row_scale
            value = gate / (1.0 + jnp.exp(-gate)) * upward
            hid[core] = value.T.astype(jnp.bfloat16)

    def down(c):
        term = sum(
            jnp.dot(
                hid[core], wd[pl.ds(core * width, width), features(c)],
                preferred_element_type=jnp.float32,
            )
            for core in range(2)
        )
        both = [term[:, fold * CW : (fold + 1) * CW].reshape(16, 1, 8, CW) for fold in range(2)]
        own[:, :, piece(c)] = jnp.concatenate(both, 1).reshape(16, 16, CW)

    def plus(m, j):
        return remote(
            sp.at[m - 1, :, lanes(j)], rp.at[m - 1, :, lanes(j)],
            ps_send.at[m // 8], ps_recv.at[m - 1, j], right[m - PARENT[m]],
        )

    def minus(m, j):
        return remote(
            sm.at[m - 1, :, lanes(j)], rm.at[m - 1, :, lanes(j)],
            ms_send.at[m // 8], ms_recv.at[m - 1, j], left[m - PARENT[m]],
        )

    sides = ((1, plus, sp, rp), (-1, minus, sm, rm))

    def pass_on(m, j):
        for sign, copy, leaving, arrived in sides:
            if not goes(m, j, sign):
                continue
            slot = slot_of(sign * m)
            value = own[slot, :, lanes(j)]
            for source in children(m):
                if goes(source, j, sign):
                    copy(source, j).wait_recv()
                    value = value + arrived[source - 1, :, lanes(j)].astype(jnp.float32)
            leaving[m - 1, :, lanes(j)] = value.astype(jnp.bfloat16)
            copy(m, j).start()

    for m in (2, 1, 4, 3, 6, 5):
        for j in range(NJ):
            arrive(m, j)
            spread(m, j)
    for name in ("wg", "wu"):
        loads[name].wait()
    for h in range(2):
        for j in chunks(h):
            arrive(7, j)
            arrive(8, j)
        for push in pushes[2 * h : 2 * h + 2]:
            push.wait_recv()
        gate_up(h)
    activate()
    loads["wd"].wait()
    for h in range(2):
        pushes[4 + h].wait_recv()
        for j in chunks(h):
            for c in range(j * NC // NJ, (j + 1) * NC // NJ):
                down(c)
            for m in (8, 7):
                pass_on(m, j)
    for m in (5, 6, 3, 4, 1, 2):
        for j in range(NJ):
            pass_on(m, j)

    alive = jnp.bitwise_and(lax.broadcasted_iota(jnp.int32, (8, CW), 0), 1) < bs[0]
    for j in range(NJ):
        for m in children(0):
            plus(m, j).wait_recv()
            minus(m, j).wait_recv()
        for c in range(j * NC // NJ, (j + 1) * NC // NJ):
            value = own[0, :, piece(c)]
            for m in children(0):
                for arrived in (rp, rm):
                    value = value + arrived[m - 1, :, piece(c)].astype(jnp.float32)
            for fold in range(2):
                place = pl.ds((2 * c + fold) * CW, CW)
                done = res[:, place] + value[8 * fold : 8 * fold + 8]
                out_ref[:, place] = jnp.where(alive, done, 0.0).astype(jnp.bfloat16)

    def sent(part, sem):
        remote(part, part, sem, sem, sib).wait_send()

    for push in pushes:
        push.wait_send()
    sent(gath.at[pl.ds(1, 15)], ag_send.at[0])
    sent(sp.at[7, :, pl.ds(0, HALF // 2)], ps_send.at[1])
    sent(sm.at[7, :, pl.ds(0, HALF // 2)], ms_send.at[1])
    sent(sp.at[pl.ds(0, 7)], ps_send.at[0])
    sent(sm.at[pl.ds(0, 7)], ms_send.at[0])


def local(
    layer_input, queries, new_keys, new_values, key_cache, value_cache, norm_gain,
    gate_weight, up_weight, down_weight, batch_sizes, cache_lengths, page_table,
):
    vmem = pl.BlockSpec(memory_space=pltpu.VMEM)
    hbm = pl.BlockSpec(memory_space=pltpu.HBM)
    width = down_weight.shape[0]
    bf16, f32 = jnp.bfloat16, jnp.float32
    dma = pltpu.SemaphoreType.DMA
    out = pl.pallas_call(
        kernel,
        out_shape=pltpu.VMEM((8, D), bf16),
        in_specs=[hbm] * 13,
        out_specs=vmem,
        scratch_shapes=[
            pltpu.SMEM((1,), jnp.int32),
            pltpu.SMEM((2,), jnp.int32),
            pltpu.SMEM((2, 16), jnp.int32),
            pltpu.VMEM((4, 2, D), bf16),
            pltpu.VMEM((4, 2, D), bf16),
            pltpu.VMEM((4, 2, KVH * HD), bf16),
            pltpu.VMEM((4, 2, KVH * HD), bf16),
            pltpu.VMEM((1, D), f32),
            pltpu.VMEM((KEYS, KVH * HD), bf16),
            pltpu.VMEM((KEYS, KVH * HD), bf16),
            pltpu.VMEM((4 * width, D), bf16),
            pltpu.VMEM((2 * width, D), bf16),
            pltpu.VMEM((8, D), f32),
            pltpu.VMEM((8, D), f32),
            pltpu.VMEM((16, 16, HALF + SCALE), bf16),
            pltpu.VMEM((4 * width, 128), f32),
            pltpu.VMEM((2, 128, width), bf16),
            pltpu.VMEM((16, 16, HALF), f32),
            pltpu.VMEM((8, 16, HALF), bf16),
            pltpu.VMEM((8, 16, HALF), bf16),
            pltpu.VMEM((8, 16, HALF), bf16),
            pltpu.VMEM((8, 16, HALF), bf16),
            dma((15,)),
            dma((6,)),
            dma((6,)),
            dma((1,)),
            dma((16, NJ)),
            dma((2,)),
            dma((8, NJ)),
            dma((2,)),
            dma((8, NJ)),
        ],
        compiler_params=pltpu.CompilerParams(
            collective_id=0, has_side_effects=True, vmem_limit_bytes=56 * 1024 * 1024
        ),
    )(
        batch_sizes,
        cache_lengths,
        page_table,
        layer_input,
        queries,
        new_keys,
        new_values,
        norm_gain.reshape(1, D),
        key_cache.reshape(POOL, KVH * HD),
        value_cache.reshape(POOL, KVH * HD),
        gate_weight.T,
        up_weight.T,
        down_weight,
    )
    return out.reshape(4, 2, D)


def solution(mesh):
    placed = (
        P(None, ("rep", "dp"), None),
        P(None, ("rep", "dp"), None),
        P(None, ("rep", "dp"), None),
        P(None, ("rep", "dp"), None),
        P(("rep", "dp"), None, None),
        P(("rep", "dp"), None, None),
        P(),
        P(None, "dp"),
        P(None, "dp"),
        P("dp", None),
        P(("rep", "dp")),
        P(("rep", "dp")),
        P(("rep", "dp"), None),
    )
    return jax.shard_map(
        local, mesh=mesh, in_specs=placed, out_specs=P(None, ("rep", "dp"), None), check_vma=False
    )
```

```python
import jax
import jax.numpy as jnp
from jax import lax
from jax.experimental import pallas as pl
from jax.experimental.pallas import tpu as pltpu
from jax.sharding import PartitionSpec as P

D = 4096
H = 32
KVH = 4
HD = 128
HALF = D // 2
NJ = 4
W = HALF // NJ
SCALE = 128
NC = 4
CW = HALF // NC
REPS = 16
POOL = 1024
KEYS = POOL + 128

PARENT = {1: 0, 2: 0, 3: 2, 4: 2, 5: 4, 6: 4, 7: 6, 8: 6}


def children(m):
    return [n for n in sorted(PARENT, reverse=True) if PARENT[n] == m]


masked = -1e30
eps = 1e-05
LOGICAL = pl.DeviceIdType.LOGICAL


def slot_of(offset):
    if offset == 8 or offset == -8:
        return 15
    return 2 * offset if offset >= 0 else -2 * offset - 1


def kernel(
    bs_in, cl_in, pt_in, li_ref, q_ref, nk_ref, nv_ref, gain_ref,
    kc_ref, vc_ref, wg_ref, wu_ref, wd_ref,
    out_ref,
    bs, cl, pt, li, q, nk, nv, gain, kb, vb, wgu, wd, rows, res, gath, acc, hid, own,
    sp, sm, rp, rm,
    lsem, w_send, w_recv, ag_send, ag_recv, ps_send, ps_recv, ms_send, ms_recv,
):
    me, rep = lax.axis_index("dp"), lax.axis_index("rep")

    def place(dp):
        return dp * REPS + rep

    steps = sorted({n - m for n, m in PARENT.items()})
    right = {step: place(lax.rem(me + 2 * step, 32)) for step in steps}
    left = {step: place(lax.rem(me + 32 - 2 * step, 32)) for step in steps}
    sib = place(me + 1 - 2 * lax.rem(me, 2))

    def remote(src, dst, send, recv, dev):
        return pltpu.make_async_remote_copy(
            src_ref=src, dst_ref=dst, send_sem=send, recv_sem=recv,
            device_id=dev, device_id_type=LOGICAL,
        )

    barrier = pltpu.get_barrier_semaphore()
    partners = [*left.values(), *right.values(), sib]
    for dev in partners:
        pl.semaphore_signal(barrier, inc=1, device_id=dev, device_id_type=LOGICAL)

    width = wd.shape[0] // 2
    pool, pairs = pl.ds(0, POOL), [pl.ds(2 * HD * p, 2 * HD) for p in range(2)]
    moves = {
        "k0": (kc_ref.at[:, pairs[0]], kb.at[pool, pairs[0]]),
        "q": (q_ref, q),
        "pt": (pt_in, pt),
        "cl": (cl_in, cl),
        "nk": (nk_ref, nk),
        "v0": (vc_ref.at[:, pairs[0]], vb.at[pool, pairs[0]]),
        "nv": (nv_ref, nv),
        "li": (li_ref, li),
        "gain": (gain_ref, gain),
        "k1": (kc_ref.at[:, pairs[1]], kb.at[pool, pairs[1]]),
        "v1": (vc_ref.at[:, pairs[1]], vb.at[pool, pairs[1]]),
        "bs": (bs_in, bs),
        "wg": (wg_ref, wgu.at[pl.ds(0, width)]),
        "wu": (wu_ref, wgu.at[pl.ds(width, width)]),
        "wd": (wd_ref, wd.at[pl.ds(0, width)]),
    }
    loads = {
        name: pltpu.make_async_copy(src, dst, lsem.at[i])
        for i, (name, (src, dst)) in enumerate(moves.items())
    }
    for load in loads.values():
        load.start()

    pl.semaphore_wait(barrier, len(partners))
    pushes = []
    for part in range(2):
        columns = pl.ds(part * D // 2, D // 2)
        for k, (src, full) in enumerate(((wg_ref, wgu), (wu_ref, wgu), (wd_ref, wd))):
            dst = full.at[pl.ds((2 + k) * width if k < 2 else width, width), columns]
            pushes.append((src.at[:, columns], dst))
    order = (0, 1, 3, 4, 2, 5)
    pushes = [
        remote(*pushes[k], w_send.at[i], w_recv.at[i], sib) for i, k in enumerate(order)
    ]
    for push in pushes:
        push.start()

    def lanes(j):
        return pl.ds(j * W, W)

    def parts(m):
        return 2 if m % 2 else NJ

    def part_lanes(m, j):
        size = HALF // parts(m)
        return pl.ds(j * size, size)

    def ag(src, dst, m, j, dev):
        size = HALF // parts(m)
        part = pl.ds(j * size, size + SCALE if j == parts(m) - 1 else size)
        return remote(
            gath.at[src, :, part], gath.at[dst, :, part], ag_send.at[0], ag_recv.at[dst, j], dev
        )

    def chunks(h):
        return range(h * NJ // 2, (h + 1) * NJ // 2)

    def goes(m, j, sign):
        return m < 8 or (j < NJ // 2) == (sign > 0)

    def spread(m, j):
        for n in children(m):
            if n % 2 and j % 2 == 0:
                continue
            part = j // 2 if n % 2 else j
            for sign, devices in ((1, right), (-1, left)):
                if goes(n, j, sign):
                    ag(slot_of(-sign * m), slot_of(-sign * n), n, part, devices[n - m]).start()

    def arrive(m, j):
        for sign in (1, -1):
            if goes(m, j, sign):
                ag(0, slot_of(-sign * m), m, j, right[1]).wait_recv()

    def stacked(ref, width):
        for s in range(4):
            rows[2 * s : 2 * s + 2, :width] = ref[s].astype(jnp.float32)
        return rows[:, :width]

    loads["pt"].wait()
    loads["cl"].wait()
    col1 = lax.broadcasted_iota(jnp.int32, (1, KEYS), 1)
    page = lax.shift_right_logical(col1, 5)
    off = jnp.bitwise_and(col1, 31)
    slot_bias = []
    for b in range(2):
        count = jnp.zeros((1, KEYS), jnp.int32)
        for i in range(16):
            count = jnp.where(page == pt[b, i], cl[b] - 32 * i, count)
        slot_bias.append(jnp.where(off < count, 0.0, masked))
    row8 = lax.broadcasted_iota(jnp.int32, (8, KEYS), 0)
    col8 = lax.broadcasted_iota(jnp.int32, (8, KEYS), 1) - POOL
    rowb = jnp.bitwise_and(row8, 1)
    bias = jnp.where(
        rowb == 0,
        jnp.broadcast_to(slot_bias[0], (8, KEYS)),
        jnp.broadcast_to(slot_bias[1], (8, KEYS)),
    )
    fresh = (
        (col8 >= 0)
        & (col8 < 8)
        & (jnp.bitwise_and(col8, 1) == rowb)
        & (lax.shift_right_arithmetic(col8, 1) <= lax.shift_right_logical(row8, 1))
    )
    bias = jnp.where(fresh, 0.0, bias)

    loads["q"].wait()
    qf = stacked(q, D)
    loads["nk"].wait()
    loads["nv"].wait()
    zeros8 = jnp.zeros((8, KVH * HD), jnp.float32)
    kb[pl.ds(POOL, 16)] = jnp.concatenate([stacked(nk, KVH * HD), zeros8], 0).astype(jnp.bfloat16)
    vb[pl.ds(POOL, 16)] = jnp.concatenate([stacked(nv, KVH * HD), zeros8], 0).astype(jnp.bfloat16)
    kb[pl.ds(POOL + 16, 112)] = jnp.zeros((112, KVH * HD), jnp.bfloat16)
    vb[pl.ds(POOL + 16, 112)] = jnp.zeros((112, KVH * HD), jnp.bfloat16)
    scale = 1.0 / jnp.sqrt(jnp.float32(HD))
    blank = jnp.zeros((64, HD), jnp.float32)
    squares = jnp.zeros((8, 1), jnp.float32)
    for pair in range(KVH // 2):
        both = [
            jnp.concatenate(
                [qf[:, (16 * pair + 8 * i + g) * HD : (16 * pair + 8 * i + g + 1) * HD] for g in range(8)], 0
            )
            for i in range(2)
        ]
        both = jnp.concatenate(
            [jnp.concatenate([both[0], blank], 1), jnp.concatenate([blank, both[1]], 1)], 0
        ).astype(jnp.bfloat16)
        these = slice(2 * pair * HD, 2 * (pair + 1) * HD)
        loads[("k0", "k1")[pair]].wait()
        scores = lax.dot_general(
            both, kb[:, these], (((1,), (1,)), ((), ())), preferred_element_type=jnp.float32
        )
        scores = (scores.reshape(16, 8, KEYS) * scale + bias[None]).reshape(128, KEYS)
        highest = jnp.max(scores, axis=-1, keepdims=True)
        expo = jnp.exp(scores - highest)
        total = jnp.sum(expo, axis=-1, keepdims=True)
        loads[("v0", "v1")[pair]].wait()
        mixed = jnp.dot(
            expo.astype(jnp.bfloat16), vb[:, these], preferred_element_type=jnp.float32
        ) / total
        attention = jnp.concatenate(
            [
                mixed[64 * i + 8 * g : 64 * i + 8 * g + 8, i * HD : (i + 1) * HD]
                for i in range(2)
                for g in range(8)
            ],
            1,
        ).astype(jnp.bfloat16).astype(jnp.float32)
        if pair == 0:
            loads["li"].wait()
            inputs = stacked(li, D)
            loads["gain"].wait()
        mine = slice(pair * D // 2, (pair + 1) * D // 2)
        residual = inputs[:, mine] + attention
        res[:, mine] = residual
        squares += jnp.sum(residual * residual, axis=-1, keepdims=True)
        row = residual * gain[:, mine]
        for c in range(NC // 2):
            both = [row[:, (2 * c + fold) * CW : (2 * c + fold + 1) * CW] for fold in range(2)]
            start = pair * HALF // 2 + c * CW
            gath[0, :, start : start + CW] = jnp.concatenate(both, 0).astype(jnp.bfloat16)
        if pair == 1:
            loads["bs"].wait()
            row_scale = jnp.broadcast_to(lax.rsqrt(squares / D + eps), (8, SCALE))
            live = jnp.bitwise_and(lax.broadcasted_iota(jnp.int32, (8, SCALE), 0), 1) < bs[0]
            row_scale = jnp.where(live, row_scale, 0.0)
            high = row_scale.astype(jnp.bfloat16).astype(jnp.float32)
            gath[0, :, HALF:] = jnp.concatenate([high, row_scale - high], 0).astype(jnp.bfloat16)
        for j in chunks(pair):
            spread(0, j)
    def piece(c):
        return pl.ds(c * CW, CW)

    def features(c):
        return pl.ds(c * 2 * CW, 2 * CW)

    def gate_up(h):
        block = gath[:, :, pl.ds(h * HALF // 2, HALF // 2)].astype(jnp.float32)
        block = block.reshape(16, 2, 8, HALF // 2)
        block = jnp.concatenate(
            [
                block[:, fold, :, c * CW : (c + 1) * CW].reshape(128, CW)
                for c in range(NC // 2)
                for fold in range(2)
            ],
            1,
        )
        term = lax.dot_general(
            wgu[:, pl.ds(h * D // 2, D // 2)], block.astype(jnp.bfloat16),
            (((1,), (1,)), ((), ())), preferred_element_type=jnp.float32,
        )
        if h == 0:
            acc[...] = term
        else:
            acc[...] += term

    def activate():
        parts = gath[:, :, pl.ds(HALF, SCALE)].astype(jnp.float32).reshape(16, 2, 8, SCALE)
        row_scale = (parts[:, 0] + parts[:, 1]).reshape(128, SCALE).T[:1]
        for core in range(2):
            gate = acc[2 * core * width : (2 * core + 1) * width] * row_scale
            upward = acc[(2 * core + 1) * width : (2 * core + 2) * width] * row_scale
            value = gate / (1.0 + jnp.exp(-gate)) * upward
            hid[core] = value.T.astype(jnp.bfloat16)

    def down(c):
        term = sum(
            jnp.dot(
                hid[core], wd[pl.ds(core * width, width), features(c)],
                preferred_element_type=jnp.float32,
            )
            for core in range(2)
        )
        both = [term[:, fold * CW : (fold + 1) * CW].reshape(16, 1, 8, CW) for fold in range(2)]
        own[:, :, piece(c)] = jnp.concatenate(both, 1).reshape(16, 16, CW)

    def plus(m, j):
        return remote(
            sp.at[m - 1, :, part_lanes(m, j)], rp.at[m - 1, :, part_lanes(m, j)],
            ps_send.at[m // 8], ps_recv.at[m - 1, j], right[m - PARENT[m]],
        )

    def minus(m, j):
        return remote(
            sm.at[m - 1, :, part_lanes(m, j)], rm.at[m - 1, :, part_lanes(m, j)],
            ms_send.at[m // 8], ms_recv.at[m - 1, j], left[m - PARENT[m]],
        )

    sides = ((1, plus, sp, rp), (-1, minus, sm, rm))

    def pass_on(m, j):
        for sign, copy, leaving, arrived in sides:
            if not goes(m, j, sign):
                continue
            here = part_lanes(m, j)
            value = own[slot_of(sign * m), :, here]
            for source in children(m):
                if not goes(source, j, sign):
                    continue
                if source % 2 == 0:
                    copy(source, j).wait_recv()
                elif j % 2 == 0:
                    copy(source, j // 2).wait_recv()
                value = value + arrived[source - 1, :, here].astype(jnp.float32)
            leaving[m - 1, :, here] = value.astype(jnp.bfloat16)
            copy(m, j).start()

    for m in (2, 1, 4, 3, 6, 5):
        for j in range(parts(m)):
            arrive(m, j)
            spread(m, j)
    for name in ("wg", "wu"):
        loads[name].wait()
    for h in range(2):
        arrive(7, h)
        for j in chunks(h):
            arrive(8, j)
        for push in pushes[2 * h : 2 * h + 2]:
            push.wait_recv()
        gate_up(h)
    activate()
    loads["wd"].wait()
    for h in range(2):
        pushes[4 + h].wait_recv()
        for j in chunks(h):
            for c in range(j * NC // NJ, (j + 1) * NC // NJ):
                down(c)
            pass_on(8, j)
        pass_on(7, h)
    for m in (5, 6, 3, 4, 1, 2):
        for j in range(parts(m)):
            pass_on(m, j)

    def sent(part, sem):
        remote(part, part, sem, sem, sib).wait_send()

    for push in pushes:
        push.wait_send()
    sent(gath.at[pl.ds(1, 15)], ag_send.at[0])
    sent(sp.at[7, :, pl.ds(0, HALF // 2)], ps_send.at[1])
    sent(sm.at[7, :, pl.ds(0, HALF // 2)], ms_send.at[1])
    sent(sp.at[pl.ds(0, 7)], ps_send.at[0])
    sent(sm.at[pl.ds(0, 7)], ms_send.at[0])

    alive = jnp.bitwise_and(lax.broadcasted_iota(jnp.int32, (8, CW), 0), 1) < bs[0]
    for j in range(NJ):
        for m in children(0):
            if m % 2 == 0 or j % 2 == 0:
                plus(m, j // 2 if m % 2 else j).wait_recv()
                minus(m, j // 2 if m % 2 else j).wait_recv()
        for c in range(j * NC // NJ, (j + 1) * NC // NJ):
            value = own[0, :, piece(c)]
            for m in children(0):
                for arrived in (rp, rm):
                    value = value + arrived[m - 1, :, piece(c)].astype(jnp.float32)
            for fold in range(2):
                place = pl.ds((2 * c + fold) * CW, CW)
                done = res[:, place] + value[8 * fold : 8 * fold + 8]
                out_ref[:, place] = jnp.where(alive, done, 0.0).astype(jnp.bfloat16)


def local(
    layer_input, queries, new_keys, new_values, key_cache, value_cache, norm_gain,
    gate_weight, up_weight, down_weight, batch_sizes, cache_lengths, page_table,
):
    vmem = pl.BlockSpec(memory_space=pltpu.VMEM)
    hbm = pl.BlockSpec(memory_space=pltpu.HBM)
    width = down_weight.shape[0]
    bf16, f32 = jnp.bfloat16, jnp.float32
    dma = pltpu.SemaphoreType.DMA
    out = pl.pallas_call(
        kernel,
        out_shape=pltpu.VMEM((8, D), bf16),
        in_specs=[hbm] * 13,
        out_specs=vmem,
        scratch_shapes=[
            pltpu.SMEM((1,), jnp.int32),
            pltpu.SMEM((2,), jnp.int32),
            pltpu.SMEM((2, 16), jnp.int32),
            pltpu.VMEM((4, 2, D), bf16),
            pltpu.VMEM((4, 2, D), bf16),
            pltpu.VMEM((4, 2, KVH * HD), bf16),
            pltpu.VMEM((4, 2, KVH * HD), bf16),
            pltpu.VMEM((1, D), f32),
            pltpu.VMEM((KEYS, KVH * HD), bf16),
            pltpu.VMEM((KEYS, KVH * HD), bf16),
            pltpu.VMEM((4 * width, D), bf16),
            pltpu.VMEM((2 * width, D), bf16),
            pltpu.VMEM((8, D), f32),
            pltpu.VMEM((8, D), f32),
            pltpu.VMEM((16, 16, HALF + SCALE), bf16),
            pltpu.VMEM((4 * width, 128), f32),
            pltpu.VMEM((2, 128, width), bf16),
            pltpu.VMEM((16, 16, HALF), f32),
            pltpu.VMEM((8, 16, HALF), bf16),
            pltpu.VMEM((8, 16, HALF), bf16),
            pltpu.VMEM((8, 16, HALF), bf16),
            pltpu.VMEM((8, 16, HALF), bf16),
            dma((15,)),
            dma((6,)),
            dma((6,)),
            dma((1,)),
            dma((16, NJ)),
            dma((2,)),
            dma((8, NJ)),
            dma((2,)),
            dma((8, NJ)),
        ],
        compiler_params=pltpu.CompilerParams(
            collective_id=0, has_side_effects=True, vmem_limit_bytes=56 * 1024 * 1024
        ),
    )(
        batch_sizes,
        cache_lengths,
        page_table,
        layer_input,
        queries,
        new_keys,
        new_values,
        norm_gain.reshape(1, D),
        key_cache.reshape(POOL, KVH * HD),
        value_cache.reshape(POOL, KVH * HD),
        gate_weight.T,
        up_weight.T,
        down_weight,
    )
    return out.reshape(4, 2, D)


def solution(mesh):
    placed = (
        P(None, ("rep", "dp"), None),
        P(None, ("rep", "dp"), None),
        P(None, ("rep", "dp"), None),
        P(None, ("rep", "dp"), None),
        P(("rep", "dp"), None, None),
        P(("rep", "dp"), None, None),
        P(),
        P(None, "dp"),
        P(None, "dp"),
        P("dp", None),
        P(("rep", "dp")),
        P(("rep", "dp")),
        P(("rep", "dp"), None),
    )
    return jax.shard_map(
        local, mesh=mesh, in_specs=placed, out_specs=P(None, ("rep", "dp"), None), check_vma=False
    )
```

```python
import jax
import jax.numpy as jnp
from jax import lax
from jax.experimental import pallas as pl
from jax.experimental.pallas import tpu as pltpu
from jax.sharding import PartitionSpec as P

D = 4096
H = 32
KVH = 4
HD = 128
HALF = D // 2
NJ = 4
W = HALF // NJ
SCALE = 128
NC = 4
CW = HALF // NC
REPS = 16
POOL = 1024
KEYS = POOL + 128

PARENT = {1: 0, 2: 0, 3: 2, 4: 2, 5: 4, 6: 4, 7: 6, 8: 6}


def children(m):
    return [n for n in sorted(PARENT, reverse=True) if PARENT[n] == m]


masked = -1e30
eps = 1e-05
LOGICAL = pl.DeviceIdType.LOGICAL


def slot_of(offset):
    if offset == 8 or offset == -8:
        return 15
    return 2 * offset if offset >= 0 else -2 * offset - 1


def kernel(
    bs_in, cl_in, pt_in, li_ref, q_ref, nk_ref, nv_ref, gain_ref,
    kc_ref, vc_ref, wg_ref, wu_ref, wd_ref,
    out_ref,
    bs, cl, pt, li, q, nk, nv, gain, kb, vb, wgu, wd, rows, res, gath, acc, hid, own,
    sp, sm, rp, rm,
    lsem, w_send, w_recv, ag_send, ag_recv, ps_send, ps_recv, ms_send, ms_recv,
):
    me, rep = lax.axis_index("dp"), lax.axis_index("rep")

    def place(dp):
        return dp * REPS + rep

    steps = sorted({n - m for n, m in PARENT.items()})
    right = {step: place(lax.rem(me + 2 * step, 32)) for step in steps}
    left = {step: place(lax.rem(me + 32 - 2 * step, 32)) for step in steps}
    sib = place(me + 1 - 2 * lax.rem(me, 2))

    def remote(src, dst, send, recv, dev):
        return pltpu.make_async_remote_copy(
            src_ref=src, dst_ref=dst, send_sem=send, recv_sem=recv,
            device_id=dev, device_id_type=LOGICAL,
        )

    barrier = pltpu.get_barrier_semaphore()
    partners = [*left.values(), *right.values(), sib]
    for dev in partners:
        pl.semaphore_signal(barrier, inc=1, device_id=dev, device_id_type=LOGICAL)

    width = wd.shape[0] // 2
    pool, pairs = pl.ds(0, POOL), [pl.ds(2 * HD * p, 2 * HD) for p in range(2)]
    moves = {
        "k0": (kc_ref.at[:, pairs[0]], kb.at[pool, pairs[0]]),
        "q": (q_ref, q),
        "pt": (pt_in, pt),
        "cl": (cl_in, cl),
        "nk": (nk_ref, nk),
        "v0": (vc_ref.at[:, pairs[0]], vb.at[pool, pairs[0]]),
        "nv": (nv_ref, nv),
        "li": (li_ref, li),
        "gain": (gain_ref, gain),
        "k1": (kc_ref.at[:, pairs[1]], kb.at[pool, pairs[1]]),
        "v1": (vc_ref.at[:, pairs[1]], vb.at[pool, pairs[1]]),
        "bs": (bs_in, bs),
        "wg": (wg_ref, wgu.at[pl.ds(0, width)]),
        "wu": (wu_ref, wgu.at[pl.ds(width, width)]),
        "wd": (wd_ref, wd.at[pl.ds(0, width)]),
    }
    loads = {
        name: pltpu.make_async_copy(src, dst, lsem.at[i])
        for i, (name, (src, dst)) in enumerate(moves.items())
    }
    for load in loads.values():
        load.start()

    pl.semaphore_wait(barrier, len(partners))
    pushes = []
    for part in range(2):
        columns = pl.ds(part * D // 2, D // 2)
        for k, (src, full) in enumerate(((wg_ref, wgu), (wu_ref, wgu), (wd_ref, wd))):
            dst = full.at[pl.ds((2 + k) * width if k < 2 else width, width), columns]
            pushes.append((src.at[:, columns], dst))
    order = (0, 1, 3, 4, 2, 5)
    pushes = [
        remote(*pushes[k], w_send.at[i], w_recv.at[i], sib) for i, k in enumerate(order)
    ]
    for push in pushes:
        push.start()

    def lanes(j):
        return pl.ds(j * W, W)

    def parts(m):
        return 2 if m % 2 else NJ

    def part_lanes(m, j):
        size = HALF // parts(m)
        return pl.ds(j * size, size)

    def ag(src, dst, m, j, dev):
        size = HALF // parts(m)
        part = pl.ds(j * size, size + SCALE if j == parts(m) - 1 else size)
        return remote(
            gath.at[src, :, part], gath.at[dst, :, part], ag_send.at[0], ag_recv.at[dst, j], dev
        )

    def chunks(h):
        return range(h * NJ // 2, (h + 1) * NJ // 2)

    def goes(m, j, sign):
        return m < 8 or (j < NJ // 2) == (sign > 0)

    def spread(m, j):
        for n in children(m):
            if n % 2 and j % 2 == 0:
                continue
            part = j // 2 if n % 2 else j
            for sign, devices in ((1, right), (-1, left)):
                if goes(n, j, sign):
                    ag(slot_of(-sign * m), slot_of(-sign * n), n, part, devices[n - m]).start()

    def arrive(m, j):
        for sign in (1, -1):
            if goes(m, j, sign):
                ag(0, slot_of(-sign * m), m, j, right[1]).wait_recv()

    def stacked(ref, width):
        for s in range(4):
            rows[2 * s : 2 * s + 2, :width] = ref[s].astype(jnp.float32)
        return rows[:, :width]

    loads["pt"].wait()
    loads["cl"].wait()
    col1 = lax.broadcasted_iota(jnp.int32, (1, KEYS), 1)
    page = lax.shift_right_logical(col1, 5)
    off = jnp.bitwise_and(col1, 31)
    slot_bias = []
    for b in range(2):
        count = jnp.zeros((1, KEYS), jnp.int32)
        for i in range(16):
            count = jnp.where(page == pt[b, i], cl[b] - 32 * i, count)
        slot_bias.append(jnp.where(off < count, 0.0, masked))
    row8 = lax.broadcasted_iota(jnp.int32, (8, KEYS), 0)
    col8 = lax.broadcasted_iota(jnp.int32, (8, KEYS), 1) - POOL
    rowb = jnp.bitwise_and(row8, 1)
    bias = jnp.where(
        rowb == 0,
        jnp.broadcast_to(slot_bias[0], (8, KEYS)),
        jnp.broadcast_to(slot_bias[1], (8, KEYS)),
    )
    fresh = (
        (col8 >= 0)
        & (col8 < 8)
        & (jnp.bitwise_and(col8, 1) == rowb)
        & (lax.shift_right_arithmetic(col8, 1) <= lax.shift_right_logical(row8, 1))
    )
    bias = jnp.where(fresh, 0.0, bias)

    loads["q"].wait()
    qf = stacked(q, D)
    loads["nk"].wait()
    loads["nv"].wait()
    zeros8 = jnp.zeros((8, KVH * HD), jnp.float32)
    kb[pl.ds(POOL, 16)] = jnp.concatenate([stacked(nk, KVH * HD), zeros8], 0).astype(jnp.bfloat16)
    vb[pl.ds(POOL, 16)] = jnp.concatenate([stacked(nv, KVH * HD), zeros8], 0).astype(jnp.bfloat16)
    kb[pl.ds(POOL + 16, 112)] = jnp.zeros((112, KVH * HD), jnp.bfloat16)
    vb[pl.ds(POOL + 16, 112)] = jnp.zeros((112, KVH * HD), jnp.bfloat16)
    scale = 1.0 / jnp.sqrt(jnp.float32(HD))
    blank = jnp.zeros((64, HD), jnp.float32)
    squares = jnp.zeros((8, 1), jnp.float32)
    for pair in range(KVH // 2):
        both = [
            jnp.concatenate(
                [qf[:, (16 * pair + 8 * i + g) * HD : (16 * pair + 8 * i + g + 1) * HD] for g in range(8)], 0
            )
            for i in range(2)
        ]
        both = jnp.concatenate(
            [jnp.concatenate([both[0], blank], 1), jnp.concatenate([blank, both[1]], 1)], 0
        ).astype(jnp.bfloat16)
        these = slice(2 * pair * HD, 2 * (pair + 1) * HD)
        loads[("k0", "k1")[pair]].wait()
        scores = lax.dot_general(
            both, kb[:, these], (((1,), (1,)), ((), ())), preferred_element_type=jnp.float32
        )
        scores = (scores.reshape(16, 8, KEYS) * scale + bias[None]).reshape(128, KEYS)
        highest = jnp.max(scores, axis=-1, keepdims=True)
        expo = jnp.exp(scores - highest)
        total = jnp.sum(expo, axis=-1, keepdims=True)
        loads[("v0", "v1")[pair]].wait()
        mixed = jnp.dot(
            expo.astype(jnp.bfloat16), vb[:, these], preferred_element_type=jnp.float32
        ) / total
        attention = jnp.concatenate(
            [
                mixed[64 * i + 8 * g : 64 * i + 8 * g + 8, i * HD : (i + 1) * HD]
                for i in range(2)
                for g in range(8)
            ],
            1,
        ).astype(jnp.bfloat16).astype(jnp.float32)
        if pair == 0:
            loads["li"].wait()
            inputs = stacked(li, D)
            loads["gain"].wait()
        mine = slice(pair * D // 2, (pair + 1) * D // 2)
        residual = inputs[:, mine] + attention
        res[:, mine] = residual
        squares += jnp.sum(residual * residual, axis=-1, keepdims=True)
        row = residual * gain[:, mine]
        for c in range(NC // 2):
            both = [row[:, (2 * c + fold) * CW : (2 * c + fold + 1) * CW] for fold in range(2)]
            start = pair * HALF // 2 + c * CW
            gath[0, :, start : start + CW] = jnp.concatenate(both, 0).astype(jnp.bfloat16)
        if pair == 1:
            loads["bs"].wait()
            row_scale = jnp.broadcast_to(lax.rsqrt(squares / D + eps), (8, SCALE))
            live = jnp.bitwise_and(lax.broadcasted_iota(jnp.int32, (8, SCALE), 0), 1) < bs[0]
            row_scale = jnp.where(live, row_scale, 0.0)
            high = row_scale.astype(jnp.bfloat16).astype(jnp.float32)
            gath[0, :, HALF:] = jnp.concatenate([high, row_scale - high], 0).astype(jnp.bfloat16)
        for j in chunks(pair):
            spread(0, j)
    def piece(c):
        return pl.ds(c * CW, CW)

    def features(c):
        return pl.ds(c * 2 * CW, 2 * CW)

    def gate_up(h):
        block = gath[:, :, pl.ds(h * HALF // 2, HALF // 2)].astype(jnp.float32)
        block = block.reshape(16, 2, 8, HALF // 2)
        block = jnp.concatenate(
            [
                block[:, fold, :, c * CW : (c + 1) * CW].reshape(128, CW)
                for c in range(NC // 2)
                for fold in range(2)
            ],
            1,
        )
        term = lax.dot_general(
            wgu[:, pl.ds(h * D // 2, D // 2)], block.astype(jnp.bfloat16),
            (((1,), (1,)), ((), ())), preferred_element_type=jnp.float32,
        )
        if h == 0:
            acc[...] = term
        else:
            acc[...] += term

    def activate():
        parts = gath[:, :, pl.ds(HALF, SCALE)].astype(jnp.float32).reshape(16, 2, 8, SCALE)
        row_scale = (parts[:, 0] + parts[:, 1]).reshape(128, SCALE).T[:1]
        for core in range(2):
            gate = acc[2 * core * width : (2 * core + 1) * width] * row_scale
            upward = acc[(2 * core + 1) * width : (2 * core + 2) * width] * row_scale
            value = gate / (1.0 + jnp.exp(-gate)) * upward
            hid[core] = value.T.astype(jnp.bfloat16)

    def down(c):
        term = sum(
            jnp.dot(
                hid[core], wd[pl.ds(core * width, width), features(c)],
                preferred_element_type=jnp.float32,
            )
            for core in range(2)
        )
        both = [term[:, fold * CW : (fold + 1) * CW].reshape(16, 1, 8, CW) for fold in range(2)]
        own[:, :, piece(c)] = jnp.concatenate(both, 1).reshape(16, 16, CW)

    def plus(m, j):
        return remote(
            sp.at[m - 1, :, part_lanes(m, j)], rp.at[m - 1, :, part_lanes(m, j)],
            ps_send.at[m // 8], ps_recv.at[m - 1, j], right[m - PARENT[m]],
        )

    def minus(m, j):
        return remote(
            sm.at[m - 1, :, part_lanes(m, j)], rm.at[m - 1, :, part_lanes(m, j)],
            ms_send.at[m // 8], ms_recv.at[m - 1, j], left[m - PARENT[m]],
        )

    sides = ((1, plus, sp, rp), (-1, minus, sm, rm))

    def pass_on(m, j):
        for sign, copy, leaving, arrived in sides:
            if not goes(m, j, sign):
                continue
            here = part_lanes(m, j)
            value = own[slot_of(sign * m), :, here]
            for source in children(m):
                if not goes(source, j, sign):
                    continue
                if source % 2 == 0:
                    copy(source, j).wait_recv()
                elif j % 2 == 0:
                    copy(source, j // 2).wait_recv()
                value = value + arrived[source - 1, :, here].astype(jnp.float32)
            leaving[m - 1, :, here] = value.astype(jnp.bfloat16)
            copy(m, j).start()

    for m in (2, 4, 6, 1, 3, 5):
        for j in range(parts(m)):
            arrive(m, j)
            spread(m, j)
    for name in ("wg", "wu"):
        loads[name].wait()
    for h in range(2):
        arrive(7, h)
        for j in chunks(h):
            arrive(8, j)
        for push in pushes[2 * h : 2 * h + 2]:
            push.wait_recv()
        gate_up(h)
    activate()
    loads["wd"].wait()
    for h in range(2):
        pushes[4 + h].wait_recv()
        for j in chunks(h):
            for c in range(j * NC // NJ, (j + 1) * NC // NJ):
                down(c)
            pass_on(8, j)
        pass_on(7, h)
    for m in (5, 6, 3, 4, 1, 2):
        for j in range(parts(m)):
            pass_on(m, j)

    def sent(part, sem):
        remote(part, part, sem, sem, sib).wait_send()

    for push in pushes:
        push.wait_send()
    sent(gath.at[pl.ds(1, 15)], ag_send.at[0])
    sent(sp.at[7, :, pl.ds(0, HALF // 2)], ps_send.at[1])
    sent(sm.at[7, :, pl.ds(0, HALF // 2)], ms_send.at[1])
    sent(sp.at[pl.ds(0, 7)], ps_send.at[0])
    sent(sm.at[pl.ds(0, 7)], ms_send.at[0])

    alive = jnp.bitwise_and(lax.broadcasted_iota(jnp.int32, (8, CW), 0), 1) < bs[0]
    for j in range(NJ):
        for m in children(0):
            if m % 2 == 0 or j % 2 == 0:
                plus(m, j // 2 if m % 2 else j).wait_recv()
                minus(m, j // 2 if m % 2 else j).wait_recv()
        for c in range(j * NC // NJ, (j + 1) * NC // NJ):
            value = own[0, :, piece(c)]
            for m in children(0):
                for arrived in (rp, rm):
                    value = value + arrived[m - 1, :, piece(c)].astype(jnp.float32)
            for fold in range(2):
                place = pl.ds((2 * c + fold) * CW, CW)
                done = res[:, place] + value[8 * fold : 8 * fold + 8]
                out_ref[:, place] = jnp.where(alive, done, 0.0).astype(jnp.bfloat16)


def local(
    layer_input, queries, new_keys, new_values, key_cache, value_cache, norm_gain,
    gate_weight, up_weight, down_weight, batch_sizes, cache_lengths, page_table,
):
    vmem = pl.BlockSpec(memory_space=pltpu.VMEM)
    hbm = pl.BlockSpec(memory_space=pltpu.HBM)
    width = down_weight.shape[0]
    bf16, f32 = jnp.bfloat16, jnp.float32
    dma = pltpu.SemaphoreType.DMA
    out = pl.pallas_call(
        kernel,
        out_shape=pltpu.VMEM((8, D), bf16),
        in_specs=[hbm] * 13,
        out_specs=vmem,
        scratch_shapes=[
            pltpu.SMEM((1,), jnp.int32),
            pltpu.SMEM((2,), jnp.int32),
            pltpu.SMEM((2, 16), jnp.int32),
            pltpu.VMEM((4, 2, D), bf16),
            pltpu.VMEM((4, 2, D), bf16),
            pltpu.VMEM((4, 2, KVH * HD), bf16),
            pltpu.VMEM((4, 2, KVH * HD), bf16),
            pltpu.VMEM((1, D), f32),
            pltpu.VMEM((KEYS, KVH * HD), bf16),
            pltpu.VMEM((KEYS, KVH * HD), bf16),
            pltpu.VMEM((4 * width, D), bf16),
            pltpu.VMEM((2 * width, D), bf16),
            pltpu.VMEM((8, D), f32),
            pltpu.VMEM((8, D), f32),
            pltpu.VMEM((16, 16, HALF + SCALE), bf16),
            pltpu.VMEM((4 * width, 128), f32),
            pltpu.VMEM((2, 128, width), bf16),
            pltpu.VMEM((16, 16, HALF), f32),
            pltpu.VMEM((8, 16, HALF), bf16),
            pltpu.VMEM((8, 16, HALF), bf16),
            pltpu.VMEM((8, 16, HALF), bf16),
            pltpu.VMEM((8, 16, HALF), bf16),
            dma((15,)),
            dma((6,)),
            dma((6,)),
            dma((1,)),
            dma((16, NJ)),
            dma((2,)),
            dma((8, NJ)),
            dma((2,)),
            dma((8, NJ)),
        ],
        compiler_params=pltpu.CompilerParams(
            collective_id=0, has_side_effects=True, vmem_limit_bytes=56 * 1024 * 1024
        ),
    )(
        batch_sizes,
        cache_lengths,
        page_table,
        layer_input,
        queries,
        new_keys,
        new_values,
        norm_gain.reshape(1, D),
        key_cache.reshape(POOL, KVH * HD),
        value_cache.reshape(POOL, KVH * HD),
        gate_weight.T,
        up_weight.T,
        down_weight,
    )
    return out.reshape(4, 2, D)


def solution(mesh):
    placed = (
        P(None, ("rep", "dp"), None),
        P(None, ("rep", "dp"), None),
        P(None, ("rep", "dp"), None),
        P(None, ("rep", "dp"), None),
        P(("rep", "dp"), None, None),
        P(("rep", "dp"), None, None),
        P(),
        P(None, "dp"),
        P(None, "dp"),
        P("dp", None),
        P(("rep", "dp")),
        P(("rep", "dp")),
        P(("rep", "dp"), None),
    )
    return jax.shard_map(
        local, mesh=mesh, in_specs=placed, out_specs=P(None, ("rep", "dp"), None), check_vma=False
    )
```

```python
import jax
import jax.numpy as jnp
from jax import lax
from jax.experimental import pallas as pl
from jax.experimental.pallas import tpu as pltpu
from jax.sharding import PartitionSpec as P

D = 4096
H = 32
KVH = 4
HD = 128
HALF = D // 2
NJ = 4
W = HALF // NJ
SCALE = 128
NC = 4
CW = HALF // NC
REPS = 16
POOL = 1024
KEYS = POOL + 128

PARENT = {1: 0, 2: 0, 3: 2, 4: 2, 5: 4, 6: 4, 7: 6, 8: 6}


def children(m):
    return [n for n in sorted(PARENT, reverse=True) if PARENT[n] == m]


masked = -1e30
eps = 1e-05
LOGICAL = pl.DeviceIdType.LOGICAL


def slot_of(offset):
    if offset == 8 or offset == -8:
        return 15
    return 2 * offset if offset >= 0 else -2 * offset - 1


def kernel(
    bs_in, cl_in, pt_in, li_ref, q_ref, nk_ref, nv_ref, gain_ref,
    kc_ref, vc_ref, wg_ref, wu_ref, wd_ref,
    out_ref,
    bs, cl, pt, li, q, nk, nv, gain, kb, vb, wgu, wd, rows, res, gath, acc, hid, own,
    sp, sm, rp, rm,
    lsem, w_send, w_recv, ag_send, ag_recv, ps_send, ps_recv, ms_send, ms_recv,
):
    me, rep = lax.axis_index("dp"), lax.axis_index("rep")

    def place(dp):
        return dp * REPS + rep

    steps = sorted({n - m for n, m in PARENT.items()})
    right = {step: place(lax.rem(me + 2 * step, 32)) for step in steps}
    left = {step: place(lax.rem(me + 32 - 2 * step, 32)) for step in steps}
    sib = place(me + 1 - 2 * lax.rem(me, 2))

    def remote(src, dst, send, recv, dev):
        return pltpu.make_async_remote_copy(
            src_ref=src, dst_ref=dst, send_sem=send, recv_sem=recv,
            device_id=dev, device_id_type=LOGICAL,
        )

    barrier = pltpu.get_barrier_semaphore()
    partners = [*left.values(), *right.values(), sib]
    for dev in partners:
        pl.semaphore_signal(barrier, inc=1, device_id=dev, device_id_type=LOGICAL)

    width = wd.shape[0] // 2
    pool, pairs = pl.ds(0, POOL), [pl.ds(2 * HD * p, 2 * HD) for p in range(2)]
    moves = {
        "k0": (kc_ref.at[:, pairs[0]], kb.at[pool, pairs[0]]),
        "q": (q_ref, q),
        "pt": (pt_in, pt),
        "cl": (cl_in, cl),
        "nk": (nk_ref, nk),
        "v0": (vc_ref.at[:, pairs[0]], vb.at[pool, pairs[0]]),
        "nv": (nv_ref, nv),
        "li": (li_ref, li),
        "gain": (gain_ref, gain),
        "k1": (kc_ref.at[:, pairs[1]], kb.at[pool, pairs[1]]),
        "v1": (vc_ref.at[:, pairs[1]], vb.at[pool, pairs[1]]),
        "bs": (bs_in, bs),
        "wg": (wg_ref, wgu.at[pl.ds(0, width)]),
        "wu": (wu_ref, wgu.at[pl.ds(width, width)]),
        "wd": (wd_ref, wd.at[pl.ds(0, width)]),
    }
    loads = {
        name: pltpu.make_async_copy(src, dst, lsem.at[i])
        for i, (name, (src, dst)) in enumerate(moves.items())
    }
    for load in loads.values():
        load.start()

    pl.semaphore_wait(barrier, len(partners))
    pushes = []
    for part in range(2):
        columns = pl.ds(part * D // 2, D // 2)
        for k, (src, full) in enumerate(((wg_ref, wgu), (wu_ref, wgu), (wd_ref, wd))):
            dst = full.at[pl.ds((2 + k) * width if k < 2 else width, width), columns]
            pushes.append((src.at[:, columns], dst))
    order = (0, 1, 3, 4, 2, 5)
    pushes = [
        remote(*pushes[k], w_send.at[i], w_recv.at[i], sib) for i, k in enumerate(order)
    ]
    for push in pushes:
        push.start()

    def lanes(j):
        return pl.ds(j * W, W)

    def parts(m):
        return 2 if m % 2 else NJ

    def part_lanes(m, j):
        size = HALF // parts(m)
        return pl.ds(j * size, size)

    def ag(src, dst, m, j, dev):
        size = HALF // parts(m)
        part = pl.ds(j * size, size + SCALE if j == parts(m) - 1 else size)
        return remote(
            gath.at[src, :, part], gath.at[dst, :, part], ag_send.at[0], ag_recv.at[dst, j], dev
        )

    def chunks(h):
        return range(h * NJ // 2, (h + 1) * NJ // 2)

    def goes(m, j, sign):
        return m < 8 or (j < NJ // 2) == (sign > 0)

    def spread(m, j):
        for n in children(m):
            if n % 2 and j % 2 == 0:
                continue
            part = j // 2 if n % 2 else j
            for sign, devices in ((1, right), (-1, left)):
                if goes(n, j, sign):
                    ag(slot_of(-sign * m), slot_of(-sign * n), n, part, devices[n - m]).start()

    def arrive(m, j):
        for sign in (1, -1):
            if goes(m, j, sign):
                ag(0, slot_of(-sign * m), m, j, right[1]).wait_recv()

    def stacked(ref, width):
        for s in range(4):
            rows[2 * s : 2 * s + 2, :width] = ref[s].astype(jnp.float32)
        return rows[:, :width]

    loads["pt"].wait()
    loads["cl"].wait()
    col1 = lax.broadcasted_iota(jnp.int32, (1, KEYS), 1)
    page = lax.shift_right_logical(col1, 5)
    off = jnp.bitwise_and(col1, 31)
    slot_bias = []
    for b in range(2):
        count = jnp.zeros((1, KEYS), jnp.int32)
        for i in range(16):
            count = jnp.where(page == pt[b, i], cl[b] - 32 * i, count)
        slot_bias.append(jnp.where(off < count, 0.0, masked))
    row8 = lax.broadcasted_iota(jnp.int32, (8, KEYS), 0)
    col8 = lax.broadcasted_iota(jnp.int32, (8, KEYS), 1) - POOL
    rowb = jnp.bitwise_and(row8, 1)
    bias = jnp.where(
        rowb == 0,
        jnp.broadcast_to(slot_bias[0], (8, KEYS)),
        jnp.broadcast_to(slot_bias[1], (8, KEYS)),
    )
    fresh = (
        (col8 >= 0)
        & (col8 < 8)
        & (jnp.bitwise_and(col8, 1) == rowb)
        & (lax.shift_right_arithmetic(col8, 1) <= lax.shift_right_logical(row8, 1))
    )
    bias = jnp.where(fresh, 0.0, bias)
    bias = jnp.concatenate([bias] * 16, 0).T

    loads["q"].wait()
    qf = stacked(q, D)
    loads["nk"].wait()
    loads["nv"].wait()
    zeros8 = jnp.zeros((8, KVH * HD), jnp.float32)
    kb[pl.ds(POOL, 16)] = jnp.concatenate([stacked(nk, KVH * HD), zeros8], 0).astype(jnp.bfloat16)
    vb[pl.ds(POOL, 16)] = jnp.concatenate([stacked(nv, KVH * HD), zeros8], 0).astype(jnp.bfloat16)
    kb[pl.ds(POOL + 16, 112)] = jnp.zeros((112, KVH * HD), jnp.bfloat16)
    vb[pl.ds(POOL + 16, 112)] = jnp.zeros((112, KVH * HD), jnp.bfloat16)
    scale = 1.0 / jnp.sqrt(jnp.float32(HD))
    blank = jnp.zeros((64, HD), jnp.float32)
    squares = jnp.zeros((8, 1), jnp.float32)
    for pair in range(KVH // 2):
        both = [
            jnp.concatenate(
                [qf[:, (16 * pair + 8 * i + g) * HD : (16 * pair + 8 * i + g + 1) * HD] for g in range(8)], 0
            )
            for i in range(2)
        ]
        both = jnp.concatenate(
            [jnp.concatenate([both[0], blank], 1), jnp.concatenate([blank, both[1]], 1)], 0
        ).astype(jnp.bfloat16)
        these = slice(2 * pair * HD, 2 * (pair + 1) * HD)
        loads[("k0", "k1")[pair]].wait()
        scores = lax.dot_general(
            kb[:, these], both, (((1,), (1,)), ((), ())), preferred_element_type=jnp.float32
        )
        scores = scores * scale + bias
        expo = jnp.exp(scores - jnp.max(scores, axis=0, keepdims=True))
        weights = expo * (1.0 / jnp.sum(expo, axis=0, keepdims=True))
        loads[("v0", "v1")[pair]].wait()
        mixed = jnp.dot(
            weights.T.astype(jnp.bfloat16), vb[:, these], preferred_element_type=jnp.float32
        )
        attention = jnp.concatenate(
            [
                mixed[64 * i + 8 * g : 64 * i + 8 * g + 8, i * HD : (i + 1) * HD]
                for i in range(2)
                for g in range(8)
            ],
            1,
        ).astype(jnp.bfloat16).astype(jnp.float32)
        if pair == 0:
            loads["li"].wait()
            inputs = stacked(li, D)
            loads["gain"].wait()
        mine = slice(pair * D // 2, (pair + 1) * D // 2)
        residual = inputs[:, mine] + attention
        res[:, mine] = residual
        squares += jnp.sum(residual * residual, axis=-1, keepdims=True)
        row = residual * gain[:, mine]
        for c in range(NC // 2):
            both = [row[:, (2 * c + fold) * CW : (2 * c + fold + 1) * CW] for fold in range(2)]
            start = pair * HALF // 2 + c * CW
            gath[0, :, start : start + CW] = jnp.concatenate(both, 0).astype(jnp.bfloat16)
        if pair == 1:
            loads["bs"].wait()
            row_scale = jnp.broadcast_to(lax.rsqrt(squares / D + eps), (8, SCALE))
            live = jnp.bitwise_and(lax.broadcasted_iota(jnp.int32, (8, SCALE), 0), 1) < bs[0]
            row_scale = jnp.where(live, row_scale, 0.0)
            high = row_scale.astype(jnp.bfloat16).astype(jnp.float32)
            gath[0, :, HALF:] = jnp.concatenate([high, row_scale - high], 0).astype(jnp.bfloat16)
        for j in chunks(pair):
            spread(0, j)
    def piece(c):
        return pl.ds(c * CW, CW)

    def features(c):
        return pl.ds(c * 2 * CW, 2 * CW)

    def gate_up(h):
        block = gath[:, :, pl.ds(h * HALF // 2, HALF // 2)].astype(jnp.float32)
        block = block.reshape(16, 2, 8, HALF // 2)
        block = jnp.concatenate(
            [
                block[:, fold, :, c * CW : (c + 1) * CW].reshape(128, CW)
                for c in range(NC // 2)
                for fold in range(2)
            ],
            1,
        )
        term = lax.dot_general(
            wgu[:, pl.ds(h * D // 2, D // 2)], block.astype(jnp.bfloat16),
            (((1,), (1,)), ((), ())), preferred_element_type=jnp.float32,
        )
        if h == 0:
            acc[...] = term
        else:
            acc[...] += term

    def activate():
        parts = gath[:, :, pl.ds(HALF, SCALE)].astype(jnp.float32).reshape(16, 2, 8, SCALE)
        row_scale = (parts[:, 0] + parts[:, 1]).reshape(128, SCALE).T[:1]
        for core in range(2):
            gate = acc[2 * core * width : (2 * core + 1) * width] * row_scale
            upward = acc[(2 * core + 1) * width : (2 * core + 2) * width] * row_scale
            value = gate / (1.0 + jnp.exp(-gate)) * upward
            hid[core] = value.T.astype(jnp.bfloat16)

    def down(c):
        term = sum(
            jnp.dot(
                hid[core], wd[pl.ds(core * width, width), features(c)],
                preferred_element_type=jnp.float32,
            )
            for core in range(2)
        )
        both = [term[:, fold * CW : (fold + 1) * CW].reshape(16, 1, 8, CW) for fold in range(2)]
        own[:, :, piece(c)] = jnp.concatenate(both, 1).reshape(16, 16, CW)

    def plus(m, j):
        return remote(
            sp.at[m - 1, :, part_lanes(m, j)], rp.at[m - 1, :, part_lanes(m, j)],
            ps_send.at[m // 8], ps_recv.at[m - 1, j], right[m - PARENT[m]],
        )

    def minus(m, j):
        return remote(
            sm.at[m - 1, :, part_lanes(m, j)], rm.at[m - 1, :, part_lanes(m, j)],
            ms_send.at[m // 8], ms_recv.at[m - 1, j], left[m - PARENT[m]],
        )

    sides = ((1, plus, sp, rp), (-1, minus, sm, rm))

    def pass_on(m, j):
        for sign, copy, leaving, arrived in sides:
            if not goes(m, j, sign):
                continue
            here = part_lanes(m, j)
            value = own[slot_of(sign * m), :, here]
            for source in children(m):
                if not goes(source, j, sign):
                    continue
                if source % 2 == 0:
                    copy(source, j).wait_recv()
                elif j % 2 == 0:
                    copy(source, j // 2).wait_recv()
                value = value + arrived[source - 1, :, here].astype(jnp.float32)
            leaving[m - 1, :, here] = value.astype(jnp.bfloat16)
            copy(m, j).start()

    for m in (2, 1, 4, 3, 6, 5):
        for j in range(parts(m)):
            arrive(m, j)
            spread(m, j)
    for name in ("wg", "wu"):
        loads[name].wait()
    for h in range(2):
        arrive(7, h)
        for j in chunks(h):
            arrive(8, j)
        for push in pushes[2 * h : 2 * h + 2]:
            push.wait_recv()
        gate_up(h)
    activate()
    loads["wd"].wait()
    for h in range(2):
        pushes[4 + h].wait_recv()
        for j in chunks(h):
            for c in range(j * NC // NJ, (j + 1) * NC // NJ):
                down(c)
            pass_on(8, j)
        pass_on(7, h)
    for m in (5, 6, 3, 4, 1, 2):
        for j in range(parts(m)):
            pass_on(m, j)

    def sent(part, sem):
        remote(part, part, sem, sem, sib).wait_send()

    for push in pushes:
        push.wait_send()
    sent(gath.at[pl.ds(1, 15)], ag_send.at[0])
    sent(sp.at[7, :, pl.ds(0, HALF // 2)], ps_send.at[1])
    sent(sm.at[7, :, pl.ds(0, HALF // 2)], ms_send.at[1])
    sent(sp.at[pl.ds(0, 7)], ps_send.at[0])
    sent(sm.at[pl.ds(0, 7)], ms_send.at[0])

    alive = jnp.bitwise_and(lax.broadcasted_iota(jnp.int32, (8, CW), 0), 1) < bs[0]
    for j in range(NJ):
        for m in children(0):
            if m % 2 == 0 or j % 2 == 0:
                plus(m, j // 2 if m % 2 else j).wait_recv()
                minus(m, j // 2 if m % 2 else j).wait_recv()
        for c in range(j * NC // NJ, (j + 1) * NC // NJ):
            value = own[0, :, piece(c)]
            for m in children(0):
                for arrived in (rp, rm):
                    value = value + arrived[m - 1, :, piece(c)].astype(jnp.float32)
            for fold in range(2):
                place = pl.ds((2 * c + fold) * CW, CW)
                done = res[:, place] + value[8 * fold : 8 * fold + 8]
                out_ref[:, place] = jnp.where(alive, done, 0.0).astype(jnp.bfloat16)


def local(
    layer_input, queries, new_keys, new_values, key_cache, value_cache, norm_gain,
    gate_weight, up_weight, down_weight, batch_sizes, cache_lengths, page_table,
):
    vmem = pl.BlockSpec(memory_space=pltpu.VMEM)
    hbm = pl.BlockSpec(memory_space=pltpu.HBM)
    width = down_weight.shape[0]
    bf16, f32 = jnp.bfloat16, jnp.float32
    dma = pltpu.SemaphoreType.DMA
    out = pl.pallas_call(
        kernel,
        out_shape=pltpu.VMEM((8, D), bf16),
        in_specs=[hbm] * 13,
        out_specs=vmem,
        scratch_shapes=[
            pltpu.SMEM((1,), jnp.int32),
            pltpu.SMEM((2,), jnp.int32),
            pltpu.SMEM((2, 16), jnp.int32),
            pltpu.VMEM((4, 2, D), bf16),
            pltpu.VMEM((4, 2, D), bf16),
            pltpu.VMEM((4, 2, KVH * HD), bf16),
            pltpu.VMEM((4, 2, KVH * HD), bf16),
            pltpu.VMEM((1, D), f32),
            pltpu.VMEM((KEYS, KVH * HD), bf16),
            pltpu.VMEM((KEYS, KVH * HD), bf16),
            pltpu.VMEM((4 * width, D), bf16),
            pltpu.VMEM((2 * width, D), bf16),
            pltpu.VMEM((8, D), f32),
            pltpu.VMEM((8, D), f32),
            pltpu.VMEM((16, 16, HALF + SCALE), bf16),
            pltpu.VMEM((4 * width, 128), f32),
            pltpu.VMEM((2, 128, width), bf16),
            pltpu.VMEM((16, 16, HALF), f32),
            pltpu.VMEM((8, 16, HALF), bf16),
            pltpu.VMEM((8, 16, HALF), bf16),
            pltpu.VMEM((8, 16, HALF), bf16),
            pltpu.VMEM((8, 16, HALF), bf16),
            dma((15,)),
            dma((6,)),
            dma((6,)),
            dma((1,)),
            dma((16, NJ)),
            dma((2,)),
            dma((8, NJ)),
            dma((2,)),
            dma((8, NJ)),
        ],
        compiler_params=pltpu.CompilerParams(
            collective_id=0, has_side_effects=True, vmem_limit_bytes=56 * 1024 * 1024
        ),
    )(
        batch_sizes,
        cache_lengths,
        page_table,
        layer_input,
        queries,
        new_keys,
        new_values,
        norm_gain.reshape(1, D),
        key_cache.reshape(POOL, KVH * HD),
        value_cache.reshape(POOL, KVH * HD),
        gate_weight.T,
        up_weight.T,
        down_weight,
    )
    return out.reshape(4, 2, D)


def solution(mesh):
    placed = (
        P(None, ("rep", "dp"), None),
        P(None, ("rep", "dp"), None),
        P(None, ("rep", "dp"), None),
        P(None, ("rep", "dp"), None),
        P(("rep", "dp"), None, None),
        P(("rep", "dp"), None, None),
        P(),
        P(None, "dp"),
        P(None, "dp"),
        P("dp", None),
        P(("rep", "dp")),
        P(("rep", "dp")),
        P(("rep", "dp"), None),
    )
    return jax.shard_map(
        local, mesh=mesh, in_specs=placed, out_specs=P(None, ("rep", "dp"), None), check_vma=False
    )
```

```python
import jax
import jax.numpy as jnp
from jax import lax
from jax.experimental import pallas as pl
from jax.experimental.pallas import tpu as pltpu
from jax.sharding import PartitionSpec as P

D = 4096
H = 32
KVH = 4
HD = 128
HALF = D // 2
NJ = 4
W = HALF // NJ
SCALE = 128
NC = 4
CW = HALF // NC
REPS = 16
POOL = 1024
KEYS = POOL + 128

PARENT = {1: 0, 2: 0, 3: 2, 4: 2, 5: 4, 6: 4, 7: 6, 8: 6}


def children(m):
    return [n for n in sorted(PARENT, reverse=True) if PARENT[n] == m]


masked = -1e30
eps = 1e-05
LOGICAL = pl.DeviceIdType.LOGICAL


def slot_of(offset):
    if offset == 8 or offset == -8:
        return 15
    return 2 * offset if offset >= 0 else -2 * offset - 1


def kernel(
    bs_in, cl_in, pt_in, li_ref, q_ref, nk_ref, nv_ref, gain_ref,
    kc_ref, vc_ref, wg_ref, wu_ref, wd_ref,
    out_ref,
    bs, cl, pt, li, q, nk, nv, gain, kb, vb, wgu, wd, rows, res, gath, acc, hid, own,
    sp, sm, rp, rm,
    lsem, w_send, w_recv, ag_send, ag_recv, ps_send, ps_recv, ms_send, ms_recv,
):
    me, rep = lax.axis_index("dp"), lax.axis_index("rep")

    def place(dp):
        return dp * REPS + rep

    steps = sorted({n - m for n, m in PARENT.items()})
    right = {step: place(lax.rem(me + 2 * step, 32)) for step in steps}
    left = {step: place(lax.rem(me + 32 - 2 * step, 32)) for step in steps}
    sib = place(me + 1 - 2 * lax.rem(me, 2))

    def remote(src, dst, send, recv, dev):
        return pltpu.make_async_remote_copy(
            src_ref=src, dst_ref=dst, send_sem=send, recv_sem=recv,
            device_id=dev, device_id_type=LOGICAL,
        )

    barrier = pltpu.get_barrier_semaphore()
    partners = [*left.values(), *right.values(), sib]
    for dev in partners:
        pl.semaphore_signal(barrier, inc=1, device_id=dev, device_id_type=LOGICAL)

    width = wd.shape[0] // 2
    pool, pairs = pl.ds(0, POOL), [pl.ds(2 * HD * p, 2 * HD) for p in range(2)]
    moves = {
        "k0": (kc_ref.at[:, pairs[0]], kb.at[pool, pairs[0]]),
        "q": (q_ref, q),
        "pt": (pt_in, pt),
        "cl": (cl_in, cl),
        "nk": (nk_ref, nk),
        "v0": (vc_ref.at[:, pairs[0]], vb.at[pool, pairs[0]]),
        "nv": (nv_ref, nv),
        "li": (li_ref, li),
        "gain": (gain_ref, gain),
        "k1": (kc_ref.at[:, pairs[1]], kb.at[pool, pairs[1]]),
        "v1": (vc_ref.at[:, pairs[1]], vb.at[pool, pairs[1]]),
        "bs": (bs_in, bs),
        "wg": (wg_ref, wgu.at[pl.ds(0, width)]),
        "wu": (wu_ref, wgu.at[pl.ds(width, width)]),
        "wd": (wd_ref, wd.at[pl.ds(0, width)]),
    }
    loads = {
        name: pltpu.make_async_copy(src, dst, lsem.at[i])
        for i, (name, (src, dst)) in enumerate(moves.items())
    }
    for load in loads.values():
        load.start()

    pl.semaphore_wait(barrier, len(partners))
    pushes = []
    for part in range(2):
        columns = pl.ds(part * D // 2, D // 2)
        for k, (src, full) in enumerate(((wg_ref, wgu), (wu_ref, wgu), (wd_ref, wd))):
            dst = full.at[pl.ds((2 + k) * width if k < 2 else width, width), columns]
            pushes.append((src.at[:, columns], dst))
    order = (0, 1, 3, 4, 2, 5)
    pushes = [
        remote(*pushes[k], w_send.at[i], w_recv.at[i], sib) for i, k in enumerate(order)
    ]
    for push in pushes:
        push.start()

    def lanes(j):
        return pl.ds(j * W, W)

    def parts(m):
        return 2 if m % 2 else NJ

    def part_lanes(m, j):
        size = HALF // parts(m)
        return pl.ds(j * size, size)

    def ag(src, dst, m, j, dev):
        size = HALF // parts(m)
        part = pl.ds(j * size, size + SCALE if j == parts(m) - 1 else size)
        return remote(
            gath.at[src, :, part], gath.at[dst, :, part], ag_send.at[0], ag_recv.at[dst, j], dev
        )

    def chunks(h):
        return range(h * NJ // 2, (h + 1) * NJ // 2)

    def goes(m, j, sign):
        return m < 8 or (j < NJ // 2) == (sign > 0)

    def spread(m, j):
        for n in children(m):
            if n % 2 and j % 2 == 0:
                continue
            part = j // 2 if n % 2 else j
            for sign, devices in ((1, right), (-1, left)):
                if goes(n, j, sign):
                    ag(slot_of(-sign * m), slot_of(-sign * n), n, part, devices[n - m]).start()

    def arrive(m, j):
        for sign in (1, -1):
            if goes(m, j, sign):
                ag(0, slot_of(-sign * m), m, j, right[1]).wait_recv()

    def stacked(ref, width):
        for s in range(4):
            rows[2 * s : 2 * s + 2, :width] = ref[s].astype(jnp.float32)
        return rows[:, :width]

    loads["pt"].wait()
    loads["cl"].wait()
    col1 = lax.broadcasted_iota(jnp.int32, (1, KEYS), 1)
    page = lax.shift_right_logical(col1, 5)
    off = jnp.bitwise_and(col1, 31)
    slot_bias = []
    for b in range(2):
        count = jnp.zeros((1, KEYS), jnp.int32)
        for i in range(16):
            count = jnp.where(page == pt[b, i], cl[b] - 32 * i, count)
        slot_bias.append(jnp.where(off < count, 0.0, masked))
    row8 = lax.broadcasted_iota(jnp.int32, (8, KEYS), 0)
    col8 = lax.broadcasted_iota(jnp.int32, (8, KEYS), 1) - POOL
    rowb = jnp.bitwise_and(row8, 1)
    bias = jnp.where(
        rowb == 0,
        jnp.broadcast_to(slot_bias[0], (8, KEYS)),
        jnp.broadcast_to(slot_bias[1], (8, KEYS)),
    )
    fresh = (
        (col8 >= 0)
        & (col8 < 8)
        & (jnp.bitwise_and(col8, 1) == rowb)
        & (lax.shift_right_arithmetic(col8, 1) <= lax.shift_right_logical(row8, 1))
    )
    bias = jnp.where(fresh, 0.0, bias)

    loads["q"].wait()
    qf = stacked(q, D)
    loads["nk"].wait()
    loads["nv"].wait()
    zeros8 = jnp.zeros((8, KVH * HD), jnp.float32)
    kb[pl.ds(POOL, 16)] = jnp.concatenate([stacked(nk, KVH * HD), zeros8], 0).astype(jnp.bfloat16)
    vb[pl.ds(POOL, 16)] = jnp.concatenate([stacked(nv, KVH * HD), zeros8], 0).astype(jnp.bfloat16)
    kb[pl.ds(POOL + 16, 112)] = jnp.zeros((112, KVH * HD), jnp.bfloat16)
    vb[pl.ds(POOL + 16, 112)] = jnp.zeros((112, KVH * HD), jnp.bfloat16)
    scale = 1.0 / jnp.sqrt(jnp.float32(HD))
    blank = jnp.zeros((64, HD), jnp.float32)
    squares = jnp.zeros((8, 1), jnp.float32)
    for pair in range(KVH // 2):
        both = [
            jnp.concatenate(
                [qf[:, (16 * pair + 8 * i + g) * HD : (16 * pair + 8 * i + g + 1) * HD] for g in range(8)], 0
            )
            for i in range(2)
        ]
        both = jnp.concatenate(
            [jnp.concatenate([both[0], blank], 1), jnp.concatenate([blank, both[1]], 1)], 0
        ).astype(jnp.bfloat16)
        these = slice(2 * pair * HD, 2 * (pair + 1) * HD)
        loads[("k0", "k1")[pair]].wait()
        scores = lax.dot_general(
            both, kb[:, these], (((1,), (1,)), ((), ())), preferred_element_type=jnp.float32
        )
        scores = (scores.reshape(16, 8, KEYS) * scale + bias[None]).reshape(128, KEYS)
        highest = jnp.max(scores, axis=-1, keepdims=True)
        expo = jnp.exp(scores - highest)
        total = jnp.sum(expo, axis=-1, keepdims=True)
        loads[("v0", "v1")[pair]].wait()
        mixed = jnp.dot(
            expo.astype(jnp.bfloat16), vb[:, these], preferred_element_type=jnp.float32
        ) / total
        attention = jnp.concatenate(
            [
                mixed[64 * i + 8 * g : 64 * i + 8 * g + 8, i * HD : (i + 1) * HD]
                for i in range(2)
                for g in range(8)
            ],
            1,
        ).astype(jnp.bfloat16).astype(jnp.float32)
        if pair == 0:
            loads["li"].wait()
            inputs = stacked(li, D)
            loads["gain"].wait()
        mine = slice(pair * D // 2, (pair + 1) * D // 2)
        residual = inputs[:, mine] + attention
        res[:, mine] = residual
        squares += jnp.sum(residual * residual, axis=-1, keepdims=True)
        row = residual * gain[:, mine]
        for c in range(NC // 2):
            both = [row[:, (2 * c + fold) * CW : (2 * c + fold + 1) * CW] for fold in range(2)]
            start = pair * HALF // 2 + c * CW
            gath[0, :, start : start + CW] = jnp.concatenate(both, 0).astype(jnp.bfloat16)
        if pair == 1:
            loads["bs"].wait()
            row_scale = jnp.broadcast_to(lax.rsqrt(squares / D + eps), (8, SCALE))
            live = jnp.bitwise_and(lax.broadcasted_iota(jnp.int32, (8, SCALE), 0), 1) < bs[0]
            row_scale = jnp.where(live, row_scale, 0.0)
            high = row_scale.astype(jnp.bfloat16).astype(jnp.float32)
            gath[0, :, HALF:] = jnp.concatenate([high, row_scale - high], 0).astype(jnp.bfloat16)
        for j in chunks(pair):
            spread(0, j)
    def piece(c):
        return pl.ds(c * CW, CW)

    def features(c):
        return pl.ds(c * 2 * CW, 2 * CW)

    def gate_up(h):
        block = gath[:, :, pl.ds(h * HALF // 2, HALF // 2)].astype(jnp.float32)
        block = block.reshape(16, 2, 8, HALF // 2)
        block = jnp.concatenate(
            [
                block[:, fold, :, c * CW : (c + 1) * CW].reshape(128, CW)
                for c in range(NC // 2)
                for fold in range(2)
            ],
            1,
        )
        term = lax.dot_general(
            wgu[:, pl.ds(h * D // 2, D // 2)], block.astype(jnp.bfloat16),
            (((1,), (1,)), ((), ())), preferred_element_type=jnp.float32,
        )
        if h == 0:
            acc[...] = term
        else:
            acc[...] += term

    def activate():
        parts = gath[:, :, pl.ds(HALF, SCALE)].astype(jnp.float32).reshape(16, 2, 8, SCALE)
        row_scale = (parts[:, 0] + parts[:, 1]).reshape(128, SCALE).T[:1]
        for core in range(2):
            gate = acc[2 * core * width : (2 * core + 1) * width] * row_scale
            upward = acc[(2 * core + 1) * width : (2 * core + 2) * width] * row_scale
            value = gate / (1.0 + jnp.exp(-gate)) * upward
            hid[core] = value.T.astype(jnp.bfloat16)

    def down(c):
        term = sum(
            jnp.dot(
                hid[core], wd[pl.ds(core * width, width), features(c)],
                preferred_element_type=jnp.float32,
            )
            for core in range(2)
        )
        both = [term[:, fold * CW : (fold + 1) * CW].reshape(16, 1, 8, CW) for fold in range(2)]
        own[:, :, piece(c)] = jnp.concatenate(both, 1).reshape(16, 16, CW)

    def plus(m, j):
        return remote(
            sp.at[m - 1, :, part_lanes(m, j)], rp.at[m - 1, :, part_lanes(m, j)],
            ps_send.at[m // 8], ps_recv.at[m - 1, j], right[m - PARENT[m]],
        )

    def minus(m, j):
        return remote(
            sm.at[m - 1, :, part_lanes(m, j)], rm.at[m - 1, :, part_lanes(m, j)],
            ms_send.at[m // 8], ms_recv.at[m - 1, j], left[m - PARENT[m]],
        )

    sides = ((1, plus, sp, rp), (-1, minus, sm, rm))

    def pass_on(m, j):
        for sign, copy, leaving, arrived in sides:
            if not goes(m, j, sign):
                continue
            here = part_lanes(m, j)
            value = own[slot_of(sign * m), :, here]
            for source in children(m):
                if not goes(source, j, sign):
                    continue
                if source % 2 == 0:
                    copy(source, j).wait_recv()
                elif j % 2 == 0:
                    copy(source, j // 2).wait_recv()
                value = value + arrived[source - 1, :, here].astype(jnp.float32)
            leaving[m - 1, :, here] = value.astype(jnp.bfloat16)
            copy(m, j).start()

    for m in (2, 1, 4, 3, 6, 5):
        for j in range(parts(m)):
            arrive(m, j)
            spread(m, j)
    for name in ("wg", "wu"):
        loads[name].wait()
    for h in range(2):
        arrive(7, h)
        for j in chunks(h):
            arrive(8, j)
        for push in pushes[2 * h : 2 * h + 2]:
            push.wait_recv()
        gate_up(h)
    activate()
    loads["wd"].wait()
    for h in range(2):
        pushes[4 + h].wait_recv()
        for j in chunks(h):
            for c in range(j * NC // NJ, (j + 1) * NC // NJ):
                down(c)
            pass_on(8, j)
        pass_on(7, h)
    for m in (5, 6, 3, 1, 4, 2):
        for j in range(parts(m)):
            pass_on(m, j)

    def sent(part, sem):
        remote(part, part, sem, sem, sib).wait_send()

    for push in pushes:
        push.wait_send()
    sent(gath.at[pl.ds(1, 15)], ag_send.at[0])
    sent(sp.at[7, :, pl.ds(0, HALF // 2)], ps_send.at[1])
    sent(sm.at[7, :, pl.ds(0, HALF // 2)], ms_send.at[1])
    sent(sp.at[pl.ds(0, 7)], ps_send.at[0])
    sent(sm.at[pl.ds(0, 7)], ms_send.at[0])

    alive = jnp.bitwise_and(lax.broadcasted_iota(jnp.int32, (8, CW), 0), 1) < bs[0]
    for j in range(NJ):
        for m in children(0):
            if m % 2 == 0 or j % 2 == 0:
                plus(m, j // 2 if m % 2 else j).wait_recv()
                minus(m, j // 2 if m % 2 else j).wait_recv()
        for c in range(j * NC // NJ, (j + 1) * NC // NJ):
            value = own[0, :, piece(c)]
            for m in children(0):
                for arrived in (rp, rm):
                    value = value + arrived[m - 1, :, piece(c)].astype(jnp.float32)
            for fold in range(2):
                place = pl.ds((2 * c + fold) * CW, CW)
                done = res[:, place] + value[8 * fold : 8 * fold + 8]
                out_ref[:, place] = jnp.where(alive, done, 0.0).astype(jnp.bfloat16)


def local(
    layer_input, queries, new_keys, new_values, key_cache, value_cache, norm_gain,
    gate_weight, up_weight, down_weight, batch_sizes, cache_lengths, page_table,
):
    vmem = pl.BlockSpec(memory_space=pltpu.VMEM)
    hbm = pl.BlockSpec(memory_space=pltpu.HBM)
    width = down_weight.shape[0]
    bf16, f32 = jnp.bfloat16, jnp.float32
    dma = pltpu.SemaphoreType.DMA
    out = pl.pallas_call(
        kernel,
        out_shape=pltpu.VMEM((8, D), bf16),
        in_specs=[hbm] * 13,
        out_specs=vmem,
        scratch_shapes=[
            pltpu.SMEM((1,), jnp.int32),
            pltpu.SMEM((2,), jnp.int32),
            pltpu.SMEM((2, 16), jnp.int32),
            pltpu.VMEM((4, 2, D), bf16),
            pltpu.VMEM((4, 2, D), bf16),
            pltpu.VMEM((4, 2, KVH * HD), bf16),
            pltpu.VMEM((4, 2, KVH * HD), bf16),
            pltpu.VMEM((1, D), f32),
            pltpu.VMEM((KEYS, KVH * HD), bf16),
            pltpu.VMEM((KEYS, KVH * HD), bf16),
            pltpu.VMEM((4 * width, D), bf16),
            pltpu.VMEM((2 * width, D), bf16),
            pltpu.VMEM((8, D), f32),
            pltpu.VMEM((8, D), f32),
            pltpu.VMEM((16, 16, HALF + SCALE), bf16),
            pltpu.VMEM((4 * width, 128), f32),
            pltpu.VMEM((2, 128, width), bf16),
            pltpu.VMEM((16, 16, HALF), f32),
            pltpu.VMEM((8, 16, HALF), bf16),
            pltpu.VMEM((8, 16, HALF), bf16),
            pltpu.VMEM((8, 16, HALF), bf16),
            pltpu.VMEM((8, 16, HALF), bf16),
            dma((15,)),
            dma((6,)),
            dma((6,)),
            dma((1,)),
            dma((16, NJ)),
            dma((2,)),
            dma((8, NJ)),
            dma((2,)),
            dma((8, NJ)),
        ],
        compiler_params=pltpu.CompilerParams(
            collective_id=0, has_side_effects=True, vmem_limit_bytes=56 * 1024 * 1024
        ),
    )(
        batch_sizes,
        cache_lengths,
        page_table,
        layer_input,
        queries,
        new_keys,
        new_values,
        norm_gain.reshape(1, D),
        key_cache.reshape(POOL, KVH * HD),
        value_cache.reshape(POOL, KVH * HD),
        gate_weight.T,
        up_weight.T,
        down_weight,
    )
    return out.reshape(4, 2, D)


def solution(mesh):
    placed = (
        P(None, ("rep", "dp"), None),
        P(None, ("rep", "dp"), None),
        P(None, ("rep", "dp"), None),
        P(None, ("rep", "dp"), None),
        P(("rep", "dp"), None, None),
        P(("rep", "dp"), None, None),
        P(),
        P(None, "dp"),
        P(None, "dp"),
        P("dp", None),
        P(("rep", "dp")),
        P(("rep", "dp")),
        P(("rep", "dp"), None),
    )
    return jax.shard_map(
        local, mesh=mesh, in_specs=placed, out_specs=P(None, ("rep", "dp"), None), check_vma=False
    )
```
